256 devices in a mesh: view: 8 (over x, y_hi), blk: 32 (over z, y_lo, core).
Axes of the slice: x: 4, y: 4 (y_hi: 2, y_lo: 2; y = y_hi * 2 + y_lo), z: 8, core: 2. Of those that a mesh axis runs over, the one named last changes fastest.
Arguments:
- estimate: float32 [32, 32, 64, 128], P('blk'), may hold values from 0.25 to 32, as said below
- observed: float32 [8, 32, 32, 64, 128], P('view', 'blk'), may hold values from 0.15 to 40, as said below
- kernels: float32 [8, 3, 63], P('view'), may hold values from 0.005 to 2, as said below
- offsets: int32 [8, 3], P('view'), may hold values from -16 to 16, as said below
Outputs:
- restored: float32 [32, 32, 64, 128], P('blk')
The draws below stay inside these ranges and needn't reach their ends.
Inputs may be any that keep to these rules, and one draw needn't show every extreme that they name: `offsets`: shifts of every view along every dimension; some entry equals 16 and some equals -16. `estimate`: positive voxel values. `observed`: positive voxel values. `kernels`: positive taps.
All inputs are finite; a program needn't handle non-finite values.
Results may differ from the reference program's by a relative error of at most 0.00016.
Values sent between devices are 32-bit elements; how exact they have to be, the bound alone decides.
No kernel may reach another device: no remote copies, remote signals or barrier semaphores. Data moves between devices by JAX's collectives and lax.ppermute only.
A program may use at most 64 MiB of HBM per device.

```python
import math
import jax
import jax.numpy as jnp
from jax import lax

BX = 64
BY = 128
Z = 32
TAPS = 63
OFF = 16
ITERS = 2
BLOCKS_Y = 4
HALF = 31
VIEWS = 8
BLOCKS = 32
BLOCKS_X = 8
X = 512
Y = 512


def draw_offsets(key, part):
    key = jax.random.fold_in(key, 7)
    first, second = jax.random.split(key)
    values = jax.random.randint(first, (VIEWS * 3,), -OFF, OFF + 1)
    order = jax.random.permutation(second, VIEWS * 3)
    values = values.at[order[0]].set(OFF).at[order[1]].set(-OFF)
    return values.reshape(VIEWS, 3).astype(jnp.int32)


def bright_spots(key, shape):
    first, second = jax.random.split(key)
    picked = jax.random.randint(first, shape, 0, 32) == 0
    factor = jnp.exp(jax.random.uniform(second, shape, jnp.float32, math.log(2.0), math.log(8.0)))
    return jnp.where(picked, factor, jnp.float32(1.0))


def draw_estimate(key, part):
    key = jax.random.fold_in(key, 11)
    first, second = jax.random.split(key, 2)
    shape = (BLOCKS, Z, BX, BY)
    base = jnp.exp(jax.random.uniform(first, shape, jnp.float32, math.log(0.5), math.log(2.0)))
    return (base * bright_spots(second, shape)).astype(jnp.float32)


def draw_observed(key, part):
    key = jax.random.fold_in(key, 13)
    first, second = jax.random.split(key, 2)
    shape = (VIEWS, BLOCKS, Z, BX, BY)
    base = jnp.exp(jax.random.uniform(first, shape, jnp.float32, math.log(0.3), math.log(3.0)))
    return (base * bright_spots(second, shape)).astype(jnp.float32)


def draw_kernels(key, part):
    key = jax.random.fold_in(key, 17)
    first, second, third = jax.random.split(key, 3)
    width = jnp.exp(jax.random.uniform(first, (VIEWS, 3, 1), jnp.float32, 0.0, math.log(2.5)))
    distance = jnp.abs(lax.broadcasted_iota(jnp.int32, (VIEWS, 3, TAPS), 2) - HALF).astype(jnp.float32)
    tail = jax.random.uniform(second, (VIEWS, 3, 1), jnp.float32, 0.05, 0.1)
    rough = jnp.exp(jax.random.uniform(third, (VIEWS, 3, TAPS), jnp.float32, math.log(0.75), math.log(1.3)))
    core = jnp.exp(-0.5 * (distance / width) ** 2)
    spread = tail * 12.0 / (12.0 + distance)
    return ((core + spread) * rough).astype(jnp.float32)


def setup_inputs(seed: int = 0) -> dict:
    seeds = jax.random.split(jax.random.key(seed), 5)
    return {
        "estimate": draw_estimate(jax.random.fold_in(seeds[4], 71), 0),
        "observed": draw_observed(jax.random.fold_in(seeds[4], 71), 0),
        "kernels": draw_kernels(jax.random.fold_in(seeds[4], 71), 0),
        "offsets": draw_offsets(jax.random.fold_in(seeds[4], 71), 0),
    }


def filter_axis(field, taps, shift, axis):
    moved = jnp.moveaxis(field, axis, -1)
    shape = moved.shape
    length = shape[-1]
    flat = moved.reshape(-1, 1, length)
    margin = HALF + OFF
    padded = jnp.pad(flat, ((0, 0), (0, 0), (margin, margin)))
    start = (OFF - shift).astype(jnp.int32)
    window = lax.dynamic_slice_in_dim(padded, start, length + 2 * HALF, 2)
    kernel = taps[::-1].reshape(1, 1, TAPS)
    result = lax.conv_general_dilated(window, kernel, (1,), "VALID", precision=lax.Precision.HIGHEST)
    return jnp.moveaxis(result.reshape(shape), -1, axis)


def operator(field, taps, shifts):
    result = filter_axis(field, taps[0], shifts[0], 1)
    result = filter_axis(result, taps[1], shifts[1], 2)
    return filter_axis(result, taps[2], shifts[2], 0)


def assemble(blocked):
    grid = blocked.reshape(BLOCKS_X, BLOCKS_Y, Z, BX, BY).transpose(2, 0, 3, 1, 4)
    return grid.reshape(Z, X, Y)


def reference(estimate, observed, kernels, offsets):
    field = assemble(estimate)
    seen = [assemble(observed[view]) for view in range(VIEWS)]
    ones = jnp.ones((Z, X, Y), jnp.float32)
    weight = jnp.zeros((Z, X, Y), jnp.float32)
    for view in range(VIEWS):
        weight = weight + operator(ones, kernels[view][:, ::-1], -offsets[view])
    for step in range(ITERS):
        total = jnp.zeros((Z, X, Y), jnp.float32)
        for view in range(VIEWS):
            blurred = operator(field, kernels[view], offsets[view])
            total = total + operator(seen[view] / blurred, kernels[view][:, ::-1], -offsets[view])
        field = field * total / weight
    blocked = field.reshape(Z, BLOCKS_X, BX, BLOCKS_Y, BY).transpose(1, 3, 0, 2, 4)
    return blocked.reshape(BLOCKS, Z, BX, BY)
```

```python
import functools
import jax
import jax.numpy as jnp
from jax import lax
from jax.experimental import pallas as pl
from jax.experimental.pallas import tpu as pltpu
from jax.sharding import PartitionSpec as P

TAPS = 63
ITERS = 2
Z, BX, BY = 32, 64, 128
HALF_Z = Z // 2
RIM = 32
SHIFT = 16
GRID = 512
F32, BF16 = jnp.float32, jnp.bfloat16
PROF = 8


def split(x):
    hi = x.astype(BF16)
    return hi, (x - hi.astype(F32)).astype(BF16)


def dot(a, b):
    return jnp.dot(a, b, preferred_element_type=F32)


def wrap_of(pos):
    return jnp.where(pos >= GRID, 1, 0) - jnp.where(pos < 0, 1, 0)


def sds(*shape, dtype=F32):
    return jax.ShapeDtypeStruct(shape, dtype)


def call(body, out_shape, *args, smem=(), scratch=(), flops=1_000_000):
    in_specs = [
        pl.BlockSpec(memory_space=pltpu.SMEM if i in smem else pltpu.VMEM)
        for i in range(len(args))
    ]
    size = sum(a.size * a.dtype.itemsize for a in (*args, *out_shape))
    return pl.pallas_call(
        body,
        out_shape=out_shape,
        in_specs=in_specs,
        out_specs=[pl.BlockSpec(memory_space=pltpu.VMEM) for _ in out_shape],
        scratch_shapes=list(scratch),
        compiler_params=pltpu.CompilerParams(vmem_limit_bytes=40 * 1024 * 1024),
        cost_estimate=pl.CostEstimate(flops=flops, bytes_accessed=size, transcendentals=0),
    )(*args)


def even_column():
    return lax.axis_index("blk") % 2 == 0


def lanes(shape):
    return lax.broadcasted_iota(jnp.int32, shape, len(shape) - 1)


def rows_of(shape):
    return lax.broadcasted_iota(jnp.int32, shape, len(shape) - 2)


def matrices_kernel(offs, rows, lxf, lxb, wyf, wyb, wrf, wrb, kzf, kzb, prof):
    block = lax.axis_index("blk")
    s = (block // 4) * BX
    cs = (block % 4) * BY
    ox, oy, oz = offs[0, 0], offs[0, 1], offs[0, 2]
    even = even_column()

    def x_band(row, adjoint):
        base = jnp.broadcast_to(rows[row : row + 1, :BY], (BX, BY))
        band = pltpu.roll(base, 1, 1, stride=1, stride_axis=0)
        m = s + lanes((BX, BY)) - RIM
        i = s + ox + rows_of((BX, BY))
        keep = (wrap_of(m + ox) == 0) if adjoint else (wrap_of(i) == wrap_of(m))
        return jnp.where(keep, band, 0.0)

    def put_x(ref, band):
        hi, lo = split(band)
        top = jnp.concatenate([hi, hi], axis=1)
        bottom = jnp.concatenate([lo, jnp.zeros_like(lo)], axis=1)
        ref[...] = jnp.concatenate([top, bottom], axis=0)

    def y_band(row, adjoint):
        count = BY + 2 * RIM
        base = jnp.broadcast_to(rows[row : row + 1, :256], (count, 256))
        band = pltpu.roll(base, 193, 1, stride=1, stride_axis=0)[:, :BY]
        m = cs + rows_of((count, BY)) - RIM
        j = cs + oy + lanes((count, BY))
        keep = (wrap_of(m + oy) == 0) if adjoint else (wrap_of(j) == wrap_of(m))
        return jnp.where(keep, band, 0.0)

    def put_y(main, rims, band):
        hi, lo = split(band[RIM : RIM + BY])
        main[...] = jnp.concatenate([hi, lo], axis=1)
        left, right = band[:RIM], band[RIM + BY :]
        first = jnp.where(even, right, left)
        second = jnp.where(even, left, right)
        rims[...] = jnp.zeros_like(rims)
        for part, side in enumerate((first, second)):
            hi, lo = split(side)
            for q in range(4):
                r = part * 128 + q * RIM
                rims[0, r : r + RIM, q * 128 : q * 128 + 128] = hi
                rims[1, r : r + RIM, q * 128 : q * 128 + 128] = lo

    def z_band(row, shift):
        amount = lax.rem(1024 - 248 - 8 * shift, 1024)
        moved = pltpu.roll(rows[...], amount, 1)[row : row + 1]
        base = jnp.broadcast_to(moved, (256, 1024))
        return pltpu.roll(base, 0, 1, stride=1, stride_axis=0)[:, :256]

    put_x(lxf, x_band(1, False))
    back_x = x_band(0, True)
    put_x(lxb, back_x)
    put_y(wyf, wrf, y_band(2, False))
    back_y = y_band(3, True)
    put_y(wyb, wrb, back_y)
    front_z = z_band(5, oz)
    kzf[0], kzf[1] = split(front_z)
    kzb[0], kzb[1] = split(z_band(4, -oz))
    turned = jnp.transpose(jnp.concatenate([back_x, jnp.zeros_like(back_x)], axis=0))
    prof_x = jnp.sum(turned, axis=0, keepdims=True)
    prof_y = jnp.sum(back_y, axis=0, keepdims=True)
    prof_z = jnp.sum(front_z, axis=0, keepdims=True)
    prof[...] = jnp.concatenate(
        [prof_x, prof_y, prof_z[:, :128], prof_z[:, 128:], jnp.zeros((4, 128), F32)], axis=0
    )


def matrices(offs, taps):
    flip = taps[:, ::-1]
    six = jnp.stack([taps[0], flip[0], taps[1], flip[1]])
    plain = jnp.pad(six, ((0, 0), (0, 1024 - TAPS)))
    deep = jnp.stack([taps[2], flip[2]])
    deep = jnp.pad(deep[:, :, None], ((0, 0), (0, 0), (0, 7))).reshape(2, 8 * TAPS)
    deep = jnp.pad(deep, ((0, 2), (0, 1024 - 8 * TAPS)))
    rows = jnp.concatenate([plain, deep], axis=0)
    outs = [
        sds(128, 256, dtype=BF16), sds(128, 256, dtype=BF16),
        sds(128, 256, dtype=BF16), sds(128, 256, dtype=BF16),
        sds(2, 256, 512, dtype=BF16), sds(2, 256, 512, dtype=BF16),
        sds(2, 256, 256, dtype=BF16), sds(2, 256, 256, dtype=BF16),
        sds(PROF, 128),
    ]
    return call(matrices_kernel, outs, offs, rows, smem=(0,))


def put_packs(first, second, planes, width):
    per = 128 // width
    even = even_column()
    for g in range(len(planes) // per):
        right = left = None
        for q in range(per):
            v = planes[g * per + q]
            r = pltpu.roll(v, (width * (q + 1)) % 128, 1) if (q + 1) % per else v
            l = pltpu.roll(v, width * q, 1) if q else v
            if q == 0:
                right, left = r, l
            else:
                there = lanes(v.shape) >= width * q
                right = jnp.where(there, r, right)
                left = jnp.where(there, l, left)
        first[g] = jnp.where(even, right, left)
        second[g] = jnp.where(even, left, right)


def put_rims(src, top, bottom, first, second):
    top[...] = src[:HALF_Z, :RIM, :]
    bottom[...] = src[:HALF_Z, BX - RIM :, :]
    put_packs(first, second, [src[HALF_Z + k] for k in range(HALF_Z)], RIM)


RIMS = [sds(HALF_Z, RIM, BY), sds(HALF_Z, RIM, BY), sds(4, BX, BY), sds(4, BX, BY)]


def start_kernel(f, obs, top, bottom, first, second, obs_top, obs_bottom):
    put_rims(f, top, bottom, first, second)
    obs_top[...] = obs[:, :SHIFT, :]
    obs_bottom[...] = obs[:, BX - SHIFT :, :]


def x_filter(mat, own, above, below, put):
    for g in range(HALF_Z // 2):
        both = []
        for k in (2 * g, 2 * g + 1):
            both.append(jnp.concatenate([above[k], own(k), below[k]], axis=0))
        hi, lo = split(jnp.concatenate(both, axis=1))
        o = dot(mat, jnp.concatenate([hi, lo], axis=0))
        o = o[:BX] + o[BX:]
        put(2 * g, o[:, :BY])
        put(2 * g + 1, o[:, BY:])


def y_filter(main, rims, own, first, second, put):
    for g in range(4):
        x = jnp.concatenate([own(4 * g + q) for q in range(4)], axis=0)
        hi, lo = split(x)
        o = dot(hi, main[...])
        o = o[:, :BY] + o[:, BY:] + dot(lo, main[:, :BY])
        hi, lo = split(jnp.concatenate([first[g], second[g]], axis=1))
        r = dot(hi, rims[0]) + dot(hi, rims[1]) + dot(lo, rims[0])
        for q in range(4):
            put(4 * g + q, o[q * BX : (q + 1) * BX] + r[:, q * BY : (q + 1) * BY])


def z_filter(mat, tiles):
    hi, lo = split(tiles)
    return dot(mat[0], hi) + dot(mat[0], lo) + dot(mat[1], hi)


def first_kernel(src, above, below, p1, p2, lx, wy, wr, xa, yb, top, bottom, q1, q2):
    def put_x(k, v):
        xa[k] = v

    def put_y(k, v):
        yb[k] = v
        top[k] = v[:RIM]
        bottom[k] = v[BX - RIM :]

    y_filter(wy, wr, lambda k: src[HALF_Z + k], p1, p2, put_y)
    x_filter(lx[...], lambda k: src[k], above, below, put_x)
    put_packs(q1, q2, [xa[k] for k in range(HALF_Z)], RIM)


def first_half(src, got, lx, wy, wr):
    outs = [
        sds(HALF_Z, BX, BY), sds(HALF_Z, BX, BY),
        sds(HALF_Z, RIM, BY), sds(HALF_Z, RIM, BY),
        sds(4, BX, BY), sds(4, BX, BY),
    ]
    return call(first_kernel, outs, src, *got, lx, wy, wr)


def second_filters(xa, yb, above, below, p1, p2, lx, wy, wr, dst):
    def put_y(k, v):
        dst[k] = v

    def put_x(k, v):
        dst[HALF_Z + k] = v

    y_filter(wy, wr, lambda k: xa[k], p1, p2, put_y)
    x_filter(lx[...], lambda k: yb[k], above, below, put_x)


def ratio_kernel(xa, yb, above, below, p1, p2, lx, wy, wr, kf, kb, obs,
                 out, top, bottom, q1, q2, tmp):
    second_filters(xa, yb, above, below, p1, p2, lx, wy, wr, tmp)
    for t in range(BX // 16):
        lo_tile = tmp[:, 16 * t : 16 * t + 8, :].reshape(256, BY)
        hi_tile = tmp[:, 16 * t + 8 : 16 * t + 16, :].reshape(256, BY)
        blurred = z_filter(kf, jnp.concatenate([lo_tile, hi_tile], axis=1))
        seen = jnp.concatenate(
            [obs[:, 16 * t : 16 * t + 8, :].reshape(256, BY),
             obs[:, 16 * t + 8 : 16 * t + 16, :].reshape(256, BY)], axis=1)
        back = z_filter(kb, seen / blurred)
        out[:, 16 * t : 16 * t + 8, :] = back[:, :BY].reshape(Z, 8, BY)
        out[:, 16 * t + 8 : 16 * t + 16, :] = back[:, BY:].reshape(Z, 8, BY)
    put_rims(out, top, bottom, q1, q2)


def ratio(xa, yb, got, lx, wy, wr, kf, kb, obs):
    outs = [sds(Z, BX, BY), *RIMS]
    return call(ratio_kernel, outs, xa, yb, *got, lx, wy, wr, kf, kb, obs,
                scratch=[pltpu.VMEM((Z, BX, BY), F32)])


def rows_kernel(offs, obs, above, below, out, q1, q2):
    ox = offs[0, 0]
    total = BX + 2 * SHIFT
    amount = lax.rem(2 * total - SHIFT - ox, total)
    planes = []
    for k in range(Z):
        wide = jnp.concatenate([above[k], obs[k], below[k]], axis=0)
        v = pltpu.roll(wide, amount, 0)[:BX]
        out[k] = v
        planes.append(v)
    put_packs(q1, q2, planes, SHIFT)


def cols_kernel(offs, obs, p1, p2, out):
    oy = offs[0, 1]
    up = oy >= 0
    odd = lax.axis_index("blk") % 2
    use_first = jnp.where(up, 0, 1) == odd
    pos = lanes((BX, BY)) + oy
    outside = (pos >= BY) | (pos < 0)
    amount = lax.rem(BY - oy, BY)
    for g in range(4):
        pack = jnp.where(use_first, p1[g], p2[g])
        for q in range(8):
            k = 8 * g + q
            side = lax.rem(2 * BY - oy - 16 * q - jnp.where(up, 0, 16), BY)
            own = pltpu.roll(obs[k], amount, 1)
            out[k] = jnp.where(outside, pltpu.roll(pack, side, 1), own)


def places(x):
    a = (x ^ (x >> 1)) & 1
    b = x >> 1
    g = x & 1
    return a, b, g


def back_kernel(with_prof, *refs):
    if with_prof:
        xa, yb, above, below, p1, p2, lx, wy, wr, prof, sa, ka, sb, kb, tmp = refs
    else:
        xa, yb, above, below, p1, p2, lx, wy, wr, sa, ka, sb, kb, tmp = refs
    second_filters(xa, yb, above, below, p1, p2, lx, wy, wr, tmp)
    a, b, _ = places(lax.axis_index("view") // 2)
    sa[:512] = tmp[pl.ds(8 * (1 - a), 8)].reshape(512, BY)
    ka[...] = tmp[pl.ds(8 * a, 8)].reshape(512, BY)
    sb[:512] = tmp[pl.ds(HALF_Z + 8 * (1 - b), 8)].reshape(512, BY)
    kb[...] = tmp[pl.ds(HALF_Z + 8 * b, 8)].reshape(512, BY)
    if with_prof:
        sa[512:] = prof[...]
        sb[512:] = prof[...]


def back(xa, yb, got, lx, wy, wr, prof):
    extra = 0 if prof is None else PROF
    outs = [sds(512 + extra, BY), sds(512, BY), sds(512 + extra, BY), sds(512, BY)]
    args = [xa, yb, *got, lx, wy, wr] + ([] if prof is None else [prof])
    return call(functools.partial(back_kernel, prof is not None), outs, *args,
                scratch=[pltpu.VMEM((Z, BX, BY), F32)])


def add_kernel(with_prof, ka, ra, kb, rb, sa, na, sb, nb):
    _, b, g = places(lax.axis_index("view") // 2)
    for keep, got, send, new, pick in ((ka, ra, sa, na, b), (kb, rb, sb, nb, g)):
        there = pl.multiple_of(256 * (1 - pick), 256)
        here = pl.multiple_of(256 * pick, 256)
        send[:256] = keep[pl.ds(there, 256)] + got[pl.ds(there, 256)]
        new[...] = keep[pl.ds(here, 256)] + got[pl.ds(here, 256)]
    if with_prof:
        sa[256:] = ra[512:]


def join_kernel(with_prof, *refs):
    if with_prof:
        na, ra, nb, rb, prof, fa, fb, out = refs
    else:
        na, ra, nb, rb, out = refs
    out[:256] = na[...] + ra[:256]
    out[256:512] = nb[...] + rb[...]
    if with_prof:
        out[512:520] = prof[...]
        out[520:528] = fa[512:]
        out[528:536] = fb[512:]
        out[536:544] = ra[256:]


def update_kernel(with_prof, *refs):
    if with_prof:
        f, mine, other, out, weight, turned = refs
    else:
        f, mine, other, weight, out = refs
    a, b, g = places(lax.axis_index("view") // 2)
    starts = (8 * a + 4 * b, HALF_Z + 8 * b + 4 * g)
    if with_prof:
        every = jnp.concatenate(
            [mine[512:], other[512:], jnp.zeros((64, 128), F32)], axis=0)
        turned[...] = jnp.transpose(every)
        outer = []
        for v in range(8):
            row = every[8 * v + 1 : 8 * v + 2]
            outer.append(turned[:BX, 8 * v : 8 * v + 1] * row)
        for half in range(2):
            for k in range(4):
                depth = starts[half] + k - half * HALF_Z
                z_row = turned[pl.ds(pl.multiple_of(8 * depth, 8), 1), :]
                total = None
                for v in range(8):
                    c = 8 * v + 2 + half
                    term = z_row[:, c : c + 1] * outer[v]
                    total = term if total is None else total + term
                r = (4 * half + k) * BX
                weight[r : r + BX] = total
    for half in range(2):
        r = 256 * half
        old = f[pl.ds(starts[half], 4)].reshape(256, BY)
        total = mine[r : r + 256] + other[r : r + 256]
        out[r : r + 256] = old * total / weight[r : r + 256]


def gather_kernel(last, own, r1, r3, a2, b2, f, *rims):
    x = lax.axis_index("view") // 2

    def place(who, va, vb):
        a, b, g = places(who)
        f[pl.ds(8 * a + 4 * b, 4)] = va.reshape(4, BX, BY)
        f[pl.ds(HALF_Z + 8 * b + 4 * g, 4)] = vb.reshape(4, BX, BY)

    place(x, own[:256], own[256:])
    place(x ^ 1, r1[:256], r1[256:])
    place(x ^ 3, r3[:256], r3[256:])
    place(x ^ 2, a2[...], b2[...])
    if not last:
        put_rims(f, *rims)


def along_rows(x, by):
    return lax.ppermute(x, "blk", [(i, (i + 4 * by) % 32) for i in range(32)])


def across(x, mask):
    return lax.ppermute(x, "blk", [(i, i ^ mask) for i in range(32)])


def view_swap(x, mask):
    return lax.ppermute(x, "view", [(i, i ^ mask) for i in range(8)])


def exchange(top, bottom, first, second):
    above = along_rows(bottom, 1)
    below = along_rows(top, -1)
    p2 = across(second, 3)
    p1 = across(first, 1)
    return above, below, p1, p2


def local(estimate, observed, kernels, offsets):
    f = estimate[0]
    seen = observed[0, 0]
    top, bottom, q1, q2, obs_top, obs_bottom = call(
        start_kernel, [*RIMS, sds(Z, SHIFT, BY), sds(Z, SHIFT, BY)], f, seen)
    got = exchange(top, bottom, q1, q2)
    obs_above = along_rows(obs_bottom, 1)
    obs_below = along_rows(obs_top, -1)
    lxf, lxb, wyf, wyb, wrf, wrb, kzf, kzb, prof = matrices(offsets, kernels[0])
    weight = obs = None
    for step in range(ITERS):
        xa, yb, top, bottom, q1, q2 = first_half(f, got, lxf, wyf, wrf)
        got = exchange(top, bottom, q1, q2)
        if step == 0:
            obs, o1, o2 = call(
                rows_kernel, [sds(Z, BX, BY), sds(4, BX, BY), sds(4, BX, BY)],
                offsets, seen, obs_above, obs_below, smem=(0,))
            o2, o1 = across(o2, 3), across(o1, 1)
            (obs,) = call(cols_kernel, [sds(Z, BX, BY)], offsets, obs, o1, o2, smem=(0,))
        r, top, bottom, q1, q2 = ratio(xa, yb, got, lxf, wyf, wrf, kzf, kzb, obs)
        got = exchange(top, bottom, q1, q2)
        xa, yb, top, bottom, q1, q2 = first_half(r, got, lxb, wyb, wrb)
        got = exchange(top, bottom, q1, q2)
        first = step == 0
        sa, ka, sb, kb = back(xa, yb, got, lxb, wyb, wrb, prof if first else None)
        ra, rb = view_swap(sa, 2), view_swap(sb, 6)
        extra = PROF if first else 0
        sa, na, sb, nb = call(
            functools.partial(add_kernel, first),
            [sds(256 + extra, BY), sds(256, BY), sds(256, BY), sds(256, BY)], ka, ra, kb, rb)
        ra2, rb2 = view_swap(sa, 6), view_swap(sb, 2)
        args = [na, ra2, nb, rb2] + ([prof, ra, rb] if first else [])
        (mine,) = call(functools.partial(join_kernel, first),
                       [sds(512 + 4 * extra, BY)], *args)
        other = view_swap(mine, 1)
        if first:
            new, weight = call(
                functools.partial(update_kernel, True), [sds(512, BY), sds(512, BY)],
                f, mine, other, scratch=[pltpu.VMEM((128, 128), F32)])
        else:
            (new,) = call(functools.partial(update_kernel, False), [sds(512, BY)],
                          f, mine, other, weight)
        r1, r3 = view_swap(new, 2), view_swap(new, 6)
        a2, b2 = view_swap(r3[:256], 2), view_swap(r1[256:], 6)
        last = step == ITERS - 1
        f, *rims = call(functools.partial(gather_kernel, last),
                        [sds(Z, BX, BY)] + ([] if last else RIMS), new, r1, r3, a2, b2)
        if not last:
            got = exchange(*rims)
    return f[None]


def solution(mesh):
    in_specs = (
        P("blk", None, None, None),
        P("view", "blk", None, None, None),
        P("view", None, None),
        P("view", None),
    )
    out_specs = P("blk", None, None, None)
    return jax.shard_map(local, mesh=mesh, in_specs=in_specs, out_specs=out_specs, check_vma=False)
```

```python
import functools
import jax
import jax.numpy as jnp
from jax import lax
from jax.experimental import pallas as pl
from jax.experimental.pallas import tpu as pltpu
from jax.sharding import PartitionSpec as P

TAPS = 63
ITERS = 2
Z, BX, BY = 32, 64, 128
HALF_Z = Z // 2
RIM = 32
SHIFT = 16
GRID = 512
F32, BF16 = jnp.float32, jnp.bfloat16
PROF = 8
ORDER = (0, 1, 3, 2)


def split(x):
    hi = x.astype(BF16)
    return hi, (x - hi.astype(F32)).astype(BF16)


def dot(a, b):
    return jnp.dot(a, b, preferred_element_type=F32)


def wrap_of(pos):
    return jnp.where(pos >= GRID, 1, 0) - jnp.where(pos < 0, 1, 0)


def sds(*shape, dtype=F32):
    return jax.ShapeDtypeStruct(shape, dtype)


def call(body, out_shape, *args, smem=(), before=(), after=(), scratch=(), flops=1_000_000):
    specs = [
        pl.BlockSpec(memory_space=pltpu.SMEM if i in smem else pltpu.VMEM)
        for i in range(len(args))
    ]
    count, lead, tail = len(args), len(before), len(after)

    def inner(*refs):
        body(*refs[lead : lead + count], *refs[lead + count + tail :])

    loose = pl.BlockSpec(memory_space=pl.ANY)
    specs = [loose] * lead + specs + [loose] * tail
    size = sum(v.size * v.dtype.itemsize for v in (*args, *out_shape))
    outs = pl.pallas_call(
        inner,
        out_shape=out_shape,
        in_specs=specs,
        out_specs=[pl.BlockSpec(memory_space=pltpu.VMEM) for _ in out_shape],
        scratch_shapes=list(scratch),
        compiler_params=pltpu.CompilerParams(vmem_limit_bytes=40 * 1024 * 1024),
        cost_estimate=pl.CostEstimate(flops=flops, bytes_accessed=size, transcendentals=0),
    )(*before, *args, *after)
    return outs if len(outs) > 1 else outs[0]


def even_column():
    return lax.axis_index("blk") % 2 == 0


def lanes(shape):
    return lax.broadcasted_iota(jnp.int32, shape, len(shape) - 1)


def rows_of(shape):
    return lax.broadcasted_iota(jnp.int32, shape, len(shape) - 2)


def tap_rows(taps, full, rows, depth=True):
    full[...] = jnp.zeros_like(full)
    full[:3, :TAPS] = taps
    x = full[...]
    hi, lo = split(x)
    mid, low = split(x - hi.astype(F32))
    parts = jnp.concatenate([hi, mid, low, jnp.zeros_like(hi)], axis=0)

    def moved(step, flip, width):
        j = lax.broadcasted_iota(jnp.int32, (BY, width), 0)
        target = (TAPS - 1 - j if flip else j) * step
        hot = jnp.where((lanes((BY, width)) == target) & (j < TAPS), 1.0, 0.0).astype(BF16)
        out = dot(parts, hot)
        return out[:8] + (out[8:16] + out[16:24])

    rows[...] = jnp.zeros_like(rows)
    flipped = moved(1, True, BY)
    rows[0:1, :BY] = x[0:1]
    rows[1:2, :BY] = flipped[0:1]
    rows[2:3, :BY] = x[1:2]
    rows[3:4, :BY] = flipped[1:2]
    if depth:
        rows[4:5, :512] = moved(8, False, 512)[2:3]
        rows[5:6, :512] = moved(8, True, 512)[2:3]


def block_start():
    block = lax.axis_index("blk")
    return (block // 4) * BX, (block % 4) * BY


def x_band(rows, row, s, ox, adjoint=False):
    base = jnp.broadcast_to(rows[row : row + 1, :BY], (BX, BY))
    band = pltpu.roll(base, 1, 1, stride=1, stride_axis=0)
    m = s + lanes((BX, BY)) - RIM
    i = s + ox + rows_of((BX, BY))
    keep = (wrap_of(m + ox) == 0) if adjoint else (wrap_of(i) == wrap_of(m))
    return jnp.where(keep, band, 0.0)


def x_band_turned(rows, row, s, ox):
    base = jnp.broadcast_to(rows[row : row + 1, :256], (BY, 256))
    band = pltpu.roll(base, 193, 1, stride=1, stride_axis=0)[:, :BY]
    m = s + rows_of((BY, BY)) - RIM
    i = s + ox + lanes((BY, BY))
    keep = (wrap_of(i) == wrap_of(m)) & (lanes((BY, BY)) < BX)
    return jnp.where(keep, band, 0.0)[:, :BX]


def y_toeplitz(rows, row):
    base = jnp.broadcast_to(rows[row : row + 1, :256], (BY + 2 * RIM, 256))
    return pltpu.roll(base, 193, 1, stride=1, stride_axis=0)[:, :BY]


def y_band(rows, row, cs, oy):
    band = y_toeplitz(rows, row)
    m = cs + rows_of(band.shape)
    j = cs + oy + RIM + lanes(band.shape)
    return jnp.where(wrap_of(j) == wrap_of(m), band, 0.0)


def y_profile(rows, row, cs, oy):
    band = y_toeplitz(rows, row)
    m = cs + rows_of(band.shape) - RIM
    return jnp.sum(jnp.where(wrap_of(m + oy) == 0, band, 0.0), axis=0, keepdims=True)


def z_band(rows, row, shift):
    amount = lax.rem(1024 - 248 - 8 * shift, 1024)
    moved = pltpu.roll(rows[...], amount, 1)[row : row + 1]
    base = jnp.broadcast_to(moved, (256, 1024))
    return pltpu.roll(base, 0, 1, stride=1, stride_axis=0)[:, :256]


def put_x(ref, band):
    hi, lo = split(band)
    top = jnp.concatenate([hi, hi], axis=1)
    bottom = jnp.concatenate([lo, jnp.zeros_like(lo)], axis=1)
    ref[...] = jnp.concatenate([top, bottom], axis=0)


def put_y(main, rims, band):
    hi, lo = split(band[:BY])
    main[...] = jnp.concatenate([hi, lo], axis=1)
    side = band[BY:]
    none = jnp.zeros_like(side)
    whole = jnp.concatenate([jnp.concatenate([side, none], axis=1),
                             jnp.concatenate([none, side], axis=1)], axis=0)
    rims[0], rims[1] = split(whole)


def own_kernel(offs, taps, lxf, wyf, wrf, kzf, kzb, note, full, rows):
    tap_rows(taps[0], full, rows)
    s, cs = block_start()
    ox, oy, oz = offs[0, 0], offs[0, 1], offs[0, 2]
    put_x(lxf, x_band(rows, 1, s, ox))
    put_y(wyf, wrf, y_band(rows, 2, cs, oy))
    front_z = z_band(rows, 5, oz)
    kzf[0], kzf[1] = split(front_z)
    kzb[0], kzb[1] = split(z_band(rows, 4, -oz))
    back_x = x_band(rows, 0, s, ox, True)
    turned = jnp.transpose(jnp.concatenate([back_x, jnp.zeros_like(back_x)], axis=0))
    prof_x = jnp.sum(turned, axis=0, keepdims=True)
    prof_y = y_profile(rows, 3, cs, oy)
    prof_z = jnp.sum(front_z, axis=0, keepdims=True)
    lane = lanes((1, BY))
    shifts = jnp.where(lane == 0, ox, jnp.where(lane == 1, oy, 0)).astype(F32)
    note[...] = jnp.concatenate(
        [full[:3], shifts, prof_x, prof_y, prof_z[:, :128], prof_z[:, 128:]], axis=0)


LX, WY = sds(128, 256, dtype=BF16), sds(128, 256, dtype=BF16)
WR, KZ = sds(2, 128, 256, dtype=BF16), sds(2, 256, 256, dtype=BF16)
LT = sds(2, 128, 256, dtype=BF16)
TAP_SCRATCH = [pltpu.VMEM((8, BY), F32), pltpu.VMEM((8, 1024), F32)]


def own_matrices(offs, taps):
    return call(own_kernel, [LX, WY, WR, KZ, KZ, sds(PROF, 128)], offs, taps, smem=(0,),
                scratch=TAP_SCRATCH)


def group_kernel(n0, n1, n2, n3, lx, wy, wr, lt, full, rows):
    s, cs = block_start()
    for j, note in enumerate((n0, n1, n2, n3)):
        tap_rows(note[:3, :TAPS], full, rows, False)
        shifts = note[3:4]
        ox = shifts[:, 0:1].astype(jnp.int32)
        oy = shifts[:, 1:2].astype(jnp.int32)
        put_x(lx.at[j], x_band(rows, 1, s, ox))
        put_y(wy.at[j], wr.at[j], y_band(rows, 2, cs, oy))
        hi, lo = split(x_band_turned(rows, 0, s, ox))
        lt[0, :, j * BX : (j + 1) * BX] = hi
        lt[1, :, j * BX : (j + 1) * BX] = lo


def group_matrices(notes):
    many = lambda v: sds(4, *v.shape, dtype=v.dtype)
    return call(group_kernel, [many(LX), many(WY), many(WR), LT], *notes, scratch=TAP_SCRATCH)


def row_rims(planes, top, bottom):
    for k, plane in enumerate(planes):
        top[k] = plane[:RIM]
        bottom[k] = plane[BX - RIM :]


def col_rims(planes, out):
    there = lanes(planes[0].shape) >= BY // 2
    for g in range(len(planes) // 2):
        out[g] = jnp.where(there, pltpu.roll(planes[2 * g + 1], BY // 2, 1), planes[2 * g])


ROWS = [sds(HALF_Z, RIM, BY), sds(HALF_Z, RIM, BY)]
COLS = [sds(HALF_Z // 2, BX, BY)]
HALF = sds(HALF_Z, BX, BY)


def planes_of(*refs, half=None):
    planes = []
    for ref in refs:
        if len(ref.shape) == 3:
            skip = 0 if half is None else half * HALF_Z
            stop = ref.shape[0] if half is None else skip + HALF_Z
            planes += [ref[k] for k in range(skip, stop)]
        else:
            planes += [ref[k * BX : (k + 1) * BX] for k in range(ref.shape[0] // BX)]
    return planes


def row_rims_kernel(half, *refs):
    row_rims(planes_of(*refs[:-2], half=half), *refs[-2:])


def col_rims_kernel(half, *refs):
    col_rims(planes_of(*refs[:-1], half=half), refs[-1])


def obs_cols_kernel(obs, out):
    col_rims(planes_of(obs), out)


def x_filter(mat, own, above, below, put):
    for g in range(HALF_Z // 2):
        both = []
        for k in (2 * g, 2 * g + 1):
            both.append(jnp.concatenate([above[k], own[k], below[k]], axis=0))
        o = x_pair(mat, jnp.concatenate(both, axis=1))
        put(2 * g, o[:, :BY])
        put(2 * g + 1, o[:, BY:])


def x_pair(mat, wide):
    hi, lo = split(wide)
    o = dot(mat[...], jnp.concatenate([hi, lo], axis=0))
    return o[:BX] + o[BX:]


def y_filter(main, rims, own, packs, put):
    for g in range(len(own) // 4):
        x = jnp.concatenate([own[4 * g + q] for q in range(4)], axis=0)
        hi, lo = split(x)
        o = dot(hi, main[...])
        o = o[:, :BY] + o[:, BY:] + dot(lo, main[:, :BY])
        hi, lo = split(jnp.concatenate([packs[2 * g], packs[2 * g + 1]], axis=0))
        r = dot(hi, rims[0]) + dot(hi, rims[1]) + dot(lo, rims[0])
        for q in range(4):
            i = q // 2 * BX
            j = q % 2 * BY
            put(4 * g + q, o[q * BX : (q + 1) * BX] + r[i : i + BX, j : j + BY])


def dot_turned(a, b):
    return lax.dot_general(a, b, (((1,), (1,)), ((), ())), preferred_element_type=F32)


def z_filter(mat, tiles):
    hi, lo = split(tiles)
    return dot(mat[0], hi) + dot(mat[0], lo) + dot(mat[1], hi)


def storer(ref, place=lambda k: k):
    def put(k, v):
        ref[place(k)] = v

    return put


def y_first_kernel(count, half, *refs):
    src, (packs, wy, wr, yb, top, bottom) = refs[:count], refs[count:]

    def put(k, v):
        yb[k] = v
        top[k] = v[:RIM]
        bottom[k] = v[BX - RIM :]

    y_filter(wy, wr, planes_of(*src, half=half), packs, put)


def x_first_kernel(count, half, *refs):
    src, (above, below, lx, xa, packs) = refs[:count], refs[count:]
    x_filter(lx, planes_of(*src, half=half), above, below, storer(xa))
    col_rims(planes_of(xa), packs)


def y_first(src, half, cols, wy, wr, **more):
    return call(functools.partial(y_first_kernel, len(src), half), [HALF, *ROWS],
                *src, cols, wy, wr, **more)


def x_first(src, half, rows, lx, **more):
    return call(functools.partial(x_first_kernel, len(src), half), [HALF, *COLS],
                *src, *rows, lx, **more)


def ratio_core(tmp, kf, kb, obs, out, sends):
    for t in range(BX // 16):
        cut = [slice(16 * t, 16 * t + 8), slice(16 * t + 8, 16 * t + 16)]
        blurred = z_filter(kf, jnp.concatenate([tmp[:, c, :].reshape(256, BY) for c in cut], axis=1))
        seen = jnp.concatenate([obs[:, c, :].reshape(256, BY) for c in cut], axis=1)
        back = z_filter(kb, seen / blurred)
        for i, c in enumerate(cut):
            out[:, c, :] = back[:, i * BY : (i + 1) * BY].reshape(Z, 8, BY)
    x = lax.axis_index("view") // 2
    for j, send in zip(ORDER, sends):
        send[...] = out[pl.ds(8 * (x ^ j), 8)]


def ratio_start_kernel(xa, yb, above, below, packs, lx, wy, wr, kf, kb, obs,
                       s0, s1, s3, s2, tmp, out):
    y_filter(wy, wr, planes_of(xa), packs, storer(tmp))
    x_filter(lx, planes_of(yb), above, below, storer(tmp, lambda k: HALF_Z + k))
    ratio_core(tmp, kf, kb, obs, out, (s0, s1, s3, s2))


def ratio_kernel(g1, g3, g2, g0, kf, kb, obs, s0, s1, s3, s2, tmp, out):
    x = lax.axis_index("view") // 2
    for j, got in zip(ORDER, (g0, g1, g3, g2)):
        tmp[pl.ds(8 * (x ^ j), 8)] = got[...]
    ratio_core(tmp, kf, kb, obs, out, (s0, s1, s3, s2))


SHARD = sds(8, BX, BY)
EDGE = sds(8, RIM, BY)
PACK = sds(4, BY, BY)
WHOLE = pltpu.VMEM((Z, BX, BY), F32)


def shard_cols_kernel(own, above, below, out):
    planes = [jnp.concatenate([above[k], own[k * BX : (k + 1) * BX], below[k]], axis=0)
              for k in range(8)]
    col_rims(planes, out)


def spread_kernel(picks, own, above, below, packs, lx, wy, wr, *refs):
    outs, mid = refs[:-1], refs[-1]
    tiles = [jnp.concatenate([above[k], own[k * BX : (k + 1) * BX], below[k]], axis=0)
             for k in range(8)]
    tiles += [packs[k] for k in range(4)]
    for g in range(6):
        hi, lo = split(jnp.concatenate(tiles[2 * g : 2 * g + 2], axis=1))
        both = jnp.concatenate([hi, lo], axis=0)
        for n, j in enumerate(picks):
            o = dot(lx[j], both)
            o = o[:BX] + o[BX:]
            mid[n, 2 * g] = o[:, :BY]
            mid[n, 2 * g + 1] = o[:, BY:]
    for n, j in enumerate(picks):
        y_filter(wy.at[j], wr.at[j], [mid[n, k] for k in range(8)],
                 [mid[n, 8 + k] for k in range(4)], storer(outs[n]))


def spread(picks, new, got, packs, mats, **more):
    return call(functools.partial(spread_kernel, picks), [SHARD] * len(picks),
                new, *got, packs, *mats[:3], **more,
                scratch=[pltpu.VMEM((len(picks), 12, BX, BY), F32)])


def collect_columns(r, w, rims, put):
    for g in range(2):
        planes = [r[4 * g + q] for q in range(4)]
        hi, lo = split(jnp.concatenate(planes, axis=0))
        o = dot_turned(hi, w[:, :BY]) + dot_turned(hi, w[:, BY:]) + dot_turned(lo, w[:, :BY])
        for q in range(4):
            put(4 * g + q, o[q * BX : (q + 1) * BX])
        pairs = [jnp.concatenate(planes[2 * i : 2 * i + 2], axis=1) for i in range(2)]
        hi, lo = split(jnp.concatenate(pairs, axis=0))
        e = dot_turned(hi, rims[0]) + dot_turned(hi, rims[1]) + dot_turned(lo, rims[0])
        for i in range(2):
            put(8 + 2 * g + i, e[i * BX : (i + 1) * BX])


def collect_first_kernel(r0, r1, r3, wy, wr, mid):
    for j, r in enumerate((r0, r1, r3)):
        def put(k, v, j=j):
            mid[k, j * BX : (j + 1) * BX] = v

        collect_columns(r, wy.at[j], wr.at[j], put)


def collect_kernel(part, r2, wy, wr, lt, main, packs, late):
    def put_late(k, v):
        late[k] = v

    collect_columns(r2, wy.at[3], wr.at[3], put_late)
    for g in range(6):
        both = [jnp.concatenate([part[k], late[k]], axis=0) for k in (2 * g, 2 * g + 1)]
        hi, lo = split(jnp.concatenate(both, axis=1))
        o = dot(lt[0], hi) + dot(lt[0], lo) + dot(lt[1], hi)
        for i in range(2):
            k = 2 * g + i
            v = o[:, i * BY : (i + 1) * BY]
            if k < 8:
                main[k] = v
            else:
                packs[k - 8] = v


def add_cols_kernel(main, packs, own, up, down):
    near = lanes((BY, BY)) < BY // 2
    for k in range(8):
        pack = packs[k // 2]
        side = pltpu.roll(pack, BY // 2, 1) if k % 2 else pack
        v = main[k] + jnp.where(near, side, 0.0)
        up[k] = v[:RIM]
        own[k * BX : (k + 1) * BX] = v[RIM : RIM + BX]
        down[k] = v[RIM + BX :]


def add_rows_kernel(own, above, below, *refs):
    out, notes = refs[-1], refs[:-1]
    for k in range(8):
        r = k * BX
        out[r : r + RIM] = own[r : r + RIM] + above[k]
        out[r + RIM : r + BX] = own[r + RIM : r + BX] + below[k]
    for j, note in enumerate(notes):
        out[512 + 8 * j : 520 + 8 * j] = note[...]


def update_kernel(first, *refs):
    if first:
        f, mine, other, out, weight, top, bottom, turned = refs
    else:
        f, mine, other, weight, out = refs
    x = lax.axis_index("view") // 2
    if first:
        every = jnp.concatenate(
            [mine[512:], other[512:], jnp.zeros((64, 128), F32)], axis=0)
        turned[...] = jnp.transpose(every)
        outer = []
        for v in range(8):
            outer.append(turned[:BX, 8 * v + 4 : 8 * v + 5] * every[8 * v + 5 : 8 * v + 6])
        late = x >= 2
        for k in range(8):
            z_row = turned[pl.ds(pl.multiple_of(64 * (x % 2) + 8 * k, 8), 1), :]
            total = None
            for v in range(8):
                c = 8 * v + 6
                term = jnp.where(late, z_row[:, c + 1 : c + 2], z_row[:, c : c + 1]) * outer[v]
                total = term if total is None else total + term
            weight[k * BX : (k + 1) * BX] = total
        old = f[pl.ds(8 * x, 8)].reshape(512, BY)
    else:
        old = f[...]
    new = old * (mine[:512] + other[:512]) / weight[...]
    out[...] = new
    if first:
        for k in range(8):
            top[k] = new[k * BX : k * BX + RIM]
            bottom[k] = new[(k + 1) * BX - RIM : (k + 1) * BX]


def gather_kernel(own, r1, r3, a2, b2, f):
    x = lax.axis_index("view") // 2
    f[pl.ds(8 * x, 8)] = own[...].reshape(8, BX, BY)
    f[pl.ds(8 * (x ^ 1), 8)] = r1[...].reshape(8, BX, BY)
    f[pl.ds(8 * (x ^ 3), 8)] = r3[...].reshape(8, BX, BY)
    f[pl.ds(8 * (x ^ 2), 4)] = a2[...].reshape(4, BX, BY)
    f[pl.ds(8 * (x ^ 2) + 4, 4)] = b2[...].reshape(4, BX, BY)


def cols_kernel(offs, obs, packs, out, top, bottom):
    shift = offs[0, 1] + RIM
    outside = lanes((BX, BY)) + shift >= BY
    for k in range(Z):
        own = pltpu.roll(obs[k], BY - shift, 1)
        side = pltpu.roll(packs[k // 2], lax.rem(2 * BY - shift - BY // 2 * (k % 2), BY), 1)
        v = jnp.where(outside, side, own)
        out[k] = v
        top[k] = v[:SHIFT]
        bottom[k] = v[BX - SHIFT :]


def rows_kernel(offs, obs, above, below, out):
    ox = offs[0, 0]
    total = BX + 2 * SHIFT
    amount = lax.rem(2 * total - SHIFT - ox, total)
    for k in range(Z):
        wide = jnp.concatenate([above[k], obs[k], below[k]], axis=0)
        out[k] = pltpu.roll(wide, amount, 0)[:BX]


def along_rows(x, by):
    return lax.ppermute(x, "blk", [(i, (i + 4 * by) % 32) for i in range(32)])


def along_cols(x, by):
    return lax.ppermute(x, "blk", [(i, i // 4 * 4 + (i + by) % 4) for i in range(32)])


def view_swap(x, mask):
    return lax.ppermute(x, "view", [(i, i ^ mask) for i in range(8)])


def send_rows(top, bottom):
    return along_rows(bottom, 1), along_rows(top, -1)


def trade(own, one, three, two):
    return own, view_swap(one, 2), view_swap(three, 6), view_swap(two, 4)


def local(estimate, observed, kernels, offsets):
    f = estimate[0]
    seen = observed[0, 0]
    cols_b = along_cols(call(functools.partial(col_rims_kernel, 1), COLS, f), -1)
    rows_a = send_rows(*call(functools.partial(row_rims_kernel, 0), ROWS, f))
    lxf, wyf, wrf, kzf, kzb, note = own_matrices(offsets, kernels)
    notes = trade(note, note, note, note)
    yb, *rims = y_first((f,), 1, cols_b, wyf, wrf)
    rows_b = send_rows(*rims)
    xa, packs = x_first((f,), 0, rows_a, lxf, before=(yb,), after=notes[1:])
    cols_a = along_cols(packs, -1)
    obs_cols = along_cols(call(obs_cols_kernel, [sds(Z // 2, BX, BY)], seen), -1)
    obs, top, bottom = call(
        cols_kernel, [sds(Z, BX, BY), sds(Z, SHIFT, BY), sds(Z, SHIFT, BY)],
        offsets, seen, obs_cols, smem=(0,), before=(xa,))
    obs = call(rows_kernel, [sds(Z, BX, BY)], offsets, obs, *send_rows(top, bottom), smem=(0,))
    parts = call(ratio_start_kernel, [SHARD] * 4, xa, yb, *rows_b, cols_a,
                 lxf, wyf, wrf, kzf, kzb, obs, scratch=[WHOLE, WHOLE])
    mats = group_matrices(notes)
    lx, wy, wr, lt = mats
    for step in range(ITERS):
        first = step == 0
        if not first:
            got = send_rows(top, bottom)
            packs = along_cols(call(shard_cols_kernel, [PACK], new, *got), -1)
            one, three = spread((1, 2), new, got, packs, mats)
            two, own = spread((3, 0), new, got, packs, mats, after=(one,))
            own, one, three, two = trade(own, one, three, two)
            parts = call(ratio_kernel, [SHARD] * 4, one, three, two, own, kzf, kzb, obs,
                         scratch=[WHOLE, WHOLE])
        own, one, three, two = trade(*parts)
        part = call(collect_first_kernel, [sds(12, 192, BY)], own, one, three, wy, wr)
        main, packs = call(collect_kernel, [sds(8, BY, BY), PACK], part, two, wy, wr, lt,
                           scratch=[pltpu.VMEM((12, BX, BY), F32)])
        own, up, down = call(add_cols_kernel, [sds(512, BY), EDGE, EDGE],
                             main, along_cols(packs, 1))
        extra = notes if first else ()
        mine = call(add_rows_kernel, [sds(512 + 8 * len(extra), BY)],
                    own, *send_rows(up, down), *extra)
        other = view_swap(mine, 1)
        if first:
            new, weight, top, bottom = call(
                functools.partial(update_kernel, True),
                [sds(512, BY), sds(512, BY), EDGE, EDGE],
                f, mine, other, scratch=[pltpu.VMEM((128, 128), F32)])
        else:
            new = call(functools.partial(update_kernel, False), [sds(512, BY)],
                       new, mine, other, weight)
    r1, r3 = view_swap(new, 2), view_swap(new, 6)
    a2, b2 = view_swap(r3[:256], 2), view_swap(r1[256:], 6)
    return call(gather_kernel, [sds(Z, BX, BY)], new, r1, r3, a2, b2)[None]


def solution(mesh):
    in_specs = (
        P("blk", None, None, None),
        P("view", "blk", None, None, None),
        P("view", None, None),
        P("view", None),
    )
    out_specs = P("blk", None, None, None)
    return jax.shard_map(local, mesh=mesh, in_specs=in_specs, out_specs=out_specs, check_vma=False)
```

```python
import functools
import jax
import jax.numpy as jnp
from jax import lax
from jax.experimental import pallas as pl
from jax.experimental.pallas import tpu as pltpu
from jax.sharding import PartitionSpec as P

TAPS = 63
ITERS = 2
Z, BX, BY = 32, 64, 128
HALF_Z = Z // 2
RIM = 32
SHIFT = 16
GRID = 512
F32, BF16 = jnp.float32, jnp.bfloat16
PROF = 8
ORDER = (0, 1, 3, 2)


def split(x):
    hi = x.astype(BF16)
    return hi, (x - hi.astype(F32)).astype(BF16)


def dot(a, b):
    return jnp.dot(a, b, preferred_element_type=F32)


def wrap_of(pos):
    return jnp.where(pos >= GRID, 1, 0) - jnp.where(pos < 0, 1, 0)


def sds(*shape, dtype=F32):
    return jax.ShapeDtypeStruct(shape, dtype)


def call(body, out_shape, *args, smem=(), before=(), after=(), scratch=(), flops=1_000_000):
    specs = [
        pl.BlockSpec(memory_space=pltpu.SMEM if i in smem else pltpu.VMEM)
        for i in range(len(args))
    ]
    count, lead, tail = len(args), len(before), len(after)

    def inner(*refs):
        body(*refs[lead : lead + count], *refs[lead + count + tail :])

    loose = pl.BlockSpec(memory_space=pl.ANY)
    specs = [loose] * lead + specs + [loose] * tail
    size = sum(v.size * v.dtype.itemsize for v in (*args, *out_shape))
    outs = pl.pallas_call(
        inner,
        out_shape=out_shape,
        in_specs=specs,
        out_specs=[pl.BlockSpec(memory_space=pltpu.VMEM) for _ in out_shape],
        scratch_shapes=list(scratch),
        compiler_params=pltpu.CompilerParams(vmem_limit_bytes=40 * 1024 * 1024),
        cost_estimate=pl.CostEstimate(flops=flops, bytes_accessed=size, transcendentals=0),
    )(*before, *args, *after)
    return outs if len(outs) > 1 else outs[0]


def even_column():
    return lax.axis_index("blk") % 2 == 0


def lanes(shape):
    return lax.broadcasted_iota(jnp.int32, shape, len(shape) - 1)


def rows_of(shape):
    return lax.broadcasted_iota(jnp.int32, shape, len(shape) - 2)


def tap_rows(taps, full, rows, depth=True):
    full[...] = jnp.zeros_like(full)
    full[:3, :TAPS] = taps
    x = full[...]
    hi, lo = split(x)
    mid, low = split(x - hi.astype(F32))
    parts = jnp.concatenate([hi, mid, low, jnp.zeros_like(hi)], axis=0)

    def moved(step, flip, width):
        j = lax.broadcasted_iota(jnp.int32, (BY, width), 0)
        target = (TAPS - 1 - j if flip else j) * step
        hot = jnp.where((lanes((BY, width)) == target) & (j < TAPS), 1.0, 0.0).astype(BF16)
        out = dot(parts, hot)
        return out[:8] + (out[8:16] + out[16:24])

    rows[...] = jnp.zeros_like(rows)
    flipped = moved(1, True, BY)
    rows[0:1, :BY] = x[0:1]
    rows[1:2, :BY] = flipped[0:1]
    rows[2:3, :BY] = x[1:2]
    rows[3:4, :BY] = flipped[1:2]
    if depth:
        rows[4:5, :512] = moved(8, False, 512)[2:3]
        rows[5:6, :512] = moved(8, True, 512)[2:3]


def block_start():
    block = lax.axis_index("blk")
    return (block // 4) * BX, (block % 4) * BY


def x_band(rows, row, s, ox, adjoint=False):
    base = jnp.broadcast_to(rows[row : row + 1, :BY], (BX, BY))
    band = pltpu.roll(base, 1, 1, stride=1, stride_axis=0)
    m = s + lanes((BX, BY)) - RIM
    i = s + ox + rows_of((BX, BY))
    keep = (wrap_of(m + ox) == 0) if adjoint else (wrap_of(i) == wrap_of(m))
    return jnp.where(keep, band, 0.0)


def x_band_turned(rows, row, s, ox):
    base = jnp.broadcast_to(rows[row : row + 1, :256], (BY, 256))
    band = pltpu.roll(base, 193, 1, stride=1, stride_axis=0)[:, :BY]
    m = s + rows_of((BY, BY)) - RIM
    i = s + ox + lanes((BY, BY))
    keep = (wrap_of(i) == wrap_of(m)) & (lanes((BY, BY)) < BX)
    return jnp.where(keep, band, 0.0)[:, :BX]


def y_toeplitz(rows, row):
    base = jnp.broadcast_to(rows[row : row + 1, :256], (BY + 2 * RIM, 256))
    return pltpu.roll(base, 193, 1, stride=1, stride_axis=0)[:, :BY]


def y_band(rows, row, cs, oy):
    band = y_toeplitz(rows, row)
    m = cs + rows_of(band.shape)
    j = cs + oy + RIM + lanes(band.shape)
    return jnp.where(wrap_of(j) == wrap_of(m), band, 0.0)


def y_profile(rows, row, cs, oy):
    band = y_toeplitz(rows, row)
    m = cs + rows_of(band.shape) - RIM
    return jnp.sum(jnp.where(wrap_of(m + oy) == 0, band, 0.0), axis=0, keepdims=True)


def z_band(rows, row, shift):
    amount = lax.rem(1024 - 248 - 8 * shift, 1024)
    moved = pltpu.roll(rows[...], amount, 1)[row : row + 1]
    base = jnp.broadcast_to(moved, (256, 1024))
    return pltpu.roll(base, 0, 1, stride=1, stride_axis=0)[:, :256]


def put_x(ref, band):
    hi, lo = split(band)
    top = jnp.concatenate([hi, hi], axis=1)
    bottom = jnp.concatenate([lo, jnp.zeros_like(lo)], axis=1)
    ref[...] = jnp.concatenate([top, bottom], axis=0)


def put_y(main, rims, band):
    hi, lo = split(band[:BY])
    main[...] = jnp.concatenate([hi, lo], axis=1)
    side = band[BY:]
    none = jnp.zeros_like(side)
    whole = jnp.concatenate([jnp.concatenate([side, none], axis=1),
                             jnp.concatenate([none, side], axis=1)], axis=0)
    rims[0], rims[1] = split(whole)


def own_kernel(offs, taps, lxf, wyf, wrf, kzf, kzb, note, full, rows):
    tap_rows(taps[0], full, rows)
    s, cs = block_start()
    ox, oy, oz = offs[0, 0], offs[0, 1], offs[0, 2]
    put_x(lxf, x_band(rows, 1, s, ox))
    put_y(wyf, wrf, y_band(rows, 2, cs, oy))
    front_z = z_band(rows, 5, oz)
    kzf[0], kzf[1] = split(front_z)
    kzb[0], kzb[1] = split(z_band(rows, 4, -oz))
    back_x = x_band(rows, 0, s, ox, True)
    turned = jnp.transpose(jnp.concatenate([back_x, jnp.zeros_like(back_x)], axis=0))
    prof_x = jnp.sum(turned, axis=0, keepdims=True)
    prof_y = y_profile(rows, 3, cs, oy)
    prof_z = jnp.sum(front_z, axis=0, keepdims=True)
    lane = lanes((1, BY))
    shifts = jnp.where(lane == 0, ox, jnp.where(lane == 1, oy, 0)).astype(F32)
    note[...] = jnp.concatenate(
        [full[:3], shifts, prof_x, prof_y, prof_z[:, :128], prof_z[:, 128:]], axis=0)


LX, WY = sds(128, 256, dtype=BF16), sds(128, 256, dtype=BF16)
WR, KZ = sds(2, 128, 256, dtype=BF16), sds(2, 256, 256, dtype=BF16)
LT = sds(2, 128, 256, dtype=BF16)
TAP_SCRATCH = [pltpu.VMEM((8, BY), F32), pltpu.VMEM((8, 1024), F32)]


def own_matrices(offs, taps, **more):
    return call(own_kernel, [LX, WY, WR, KZ, KZ, sds(PROF, 128)], offs, taps, smem=(0,),
                scratch=TAP_SCRATCH, **more)


def view_matrices(note, lx, wy, wr, lt, j, full, rows):
    s, cs = block_start()
    tap_rows(note[:3, :TAPS], full, rows, False)
    shifts = note[3:4]
    ox = shifts[:, 0:1].astype(jnp.int32)
    oy = shifts[:, 1:2].astype(jnp.int32)
    put_x(lx, x_band(rows, 1, s, ox))
    put_y(wy, wr, y_band(rows, 2, cs, oy))
    hi, lo = split(x_band_turned(rows, 0, s, ox))
    lt[0, :, j * BX : (j + 1) * BX] = hi
    lt[1, :, j * BX : (j + 1) * BX] = lo


def near_matrices_kernel(note, m1, m3, lx, wy, wr, lt, full, rows):
    lt[...] = jnp.zeros_like(lt)
    for j, ref in enumerate((note, m1, m3)):
        one = ref[...] if j == 0 else ref[512:]
        view_matrices(one, lx.at[j], wy.at[j], wr.at[j], lt, j, full, rows)


def far_matrices_kernel(m2, old, lx, wy, wr, lt, full, rows):
    lt[...] = old[...]
    view_matrices(m2[512:], lx.at[0], wy.at[0], wr.at[0], lt, 3, full, rows)


def many(count):
    return [sds(count, *v.shape, dtype=v.dtype) for v in (LX, WY, WR)] + [LT]


def row_rims(planes, top, bottom):
    for k, plane in enumerate(planes):
        top[k] = plane[:RIM]
        bottom[k] = plane[BX - RIM :]


def col_rims(planes, out):
    there = lanes(planes[0].shape) >= BY // 2
    for g in range(len(planes) // 2):
        out[g] = jnp.where(there, pltpu.roll(planes[2 * g + 1], BY // 2, 1), planes[2 * g])


ROWS = [sds(HALF_Z, RIM, BY), sds(HALF_Z, RIM, BY)]
COLS = [sds(HALF_Z // 2, BX, BY)]
HALF = sds(HALF_Z, BX, BY)


def planes_of(*refs, half=None):
    planes = []
    for ref in refs:
        if len(ref.shape) == 3:
            skip = 0 if half is None else half * HALF_Z
            stop = ref.shape[0] if half is None else skip + HALF_Z
            planes += [ref[k] for k in range(skip, stop)]
        else:
            planes += [ref[k * BX : (k + 1) * BX] for k in range(ref.shape[0] // BX)]
    return planes


def row_rims_kernel(half, *refs):
    row_rims(planes_of(*refs[:-2], half=half), *refs[-2:])


def col_rims_kernel(half, *refs):
    col_rims(planes_of(*refs[:-1], half=half), refs[-1])


def obs_cols_kernel(obs, out):
    col_rims(planes_of(obs), out)


def x_filter(mat, own, above, below, put):
    for g in range(HALF_Z // 2):
        both = []
        for k in (2 * g, 2 * g + 1):
            both.append(jnp.concatenate([above[k], own[k], below[k]], axis=0))
        o = x_pair(mat, jnp.concatenate(both, axis=1))
        put(2 * g, o[:, :BY])
        put(2 * g + 1, o[:, BY:])


def x_pair(mat, wide):
    hi, lo = split(wide)
    o = dot(mat[...], jnp.concatenate([hi, lo], axis=0))
    return o[:BX] + o[BX:]


def y_filter(main, rims, own, packs, put):
    for g in range(len(own) // 4):
        x = jnp.concatenate([own[4 * g + q] for q in range(4)], axis=0)
        hi, lo = split(x)
        o = dot(hi, main[...])
        o = o[:, :BY] + o[:, BY:] + dot(lo, main[:, :BY])
        hi, lo = split(jnp.concatenate([packs[2 * g], packs[2 * g + 1]], axis=0))
        r = dot(hi, rims[0]) + dot(hi, rims[1]) + dot(lo, rims[0])
        for q in range(4):
            i = q // 2 * BX
            j = q % 2 * BY
            put(4 * g + q, o[q * BX : (q + 1) * BX] + r[i : i + BX, j : j + BY])


def dot_turned(a, b):
    return lax.dot_general(a, b, (((1,), (1,)), ((), ())), preferred_element_type=F32)


def z_filter(mat, tiles):
    hi, lo = split(tiles)
    return dot(mat[0], hi) + dot(mat[0], lo) + dot(mat[1], hi)


def storer(ref, place=lambda k: k):
    def put(k, v):
        ref[place(k)] = v

    return put


def y_first_kernel(count, half, *refs):
    src, (packs, wy, wr, yb, top, bottom) = refs[:count], refs[count:]

    def put(k, v):
        yb[k] = v
        top[k] = v[:RIM]
        bottom[k] = v[BX - RIM :]

    y_filter(wy, wr, planes_of(*src, half=half), packs, put)


def x_first_kernel(count, half, *refs):
    src, (above, below, lx, xa, packs) = refs[:count], refs[count:]
    x_filter(lx, planes_of(*src, half=half), above, below, storer(xa))
    col_rims(planes_of(xa), packs)


def y_first(src, half, cols, wy, wr, **more):
    return call(functools.partial(y_first_kernel, len(src), half), [HALF, *ROWS],
                *src, cols, wy, wr, **more)


def x_first(src, half, rows, lx, **more):
    return call(functools.partial(x_first_kernel, len(src), half), [HALF, *COLS],
                *src, *rows, lx, **more)


def ratio_core(load, kf, kb, obs, out, sends):
    for t in range(BX // 16):
        cut = [slice(16 * t, 16 * t + 8), slice(16 * t + 8, 16 * t + 16)]
        blurred = z_filter(kf, jnp.concatenate([load(c) for c in cut], axis=1))
        seen = jnp.concatenate([obs[:, c, :].reshape(256, BY) for c in cut], axis=1)
        back = z_filter(kb, seen / blurred)
        for i, c in enumerate(cut):
            out[:, c, :] = back[:, i * BY : (i + 1) * BY].reshape(Z, 8, BY)
    x = lax.axis_index("view") // 2
    for j, send in zip(ORDER, sends):
        send[:512] = out[pl.ds(8 * (x ^ j), 8)].reshape(512, BY)


def second_x_kernel(yb, above, below, lx, out):
    x_filter(lx, planes_of(yb), above, below, storer(out))


def second_y_kernel(xa, packs, wy, wr, out):
    y_filter(wy, wr, planes_of(xa), packs, storer(out))


def ratio_start_kernel(ga, gb, kf, kb, obs, note, s0, s1, s3, s2, out):
    def load(c):
        return jnp.concatenate([ga[:, c, :], gb[:, c, :]], axis=0).reshape(256, BY)

    ratio_core(load, kf, kb, obs, out, (s0, s1, s3, s2))
    for send in (s1, s3, s2):
        send[512:] = note[...]


def ratio_kernel(g1, g3, g2, g0, kf, kb, obs, s0, s1, s3, s2, tmp, out):
    x = lax.axis_index("view") // 2
    for j, got in zip(ORDER, (g0, g1, g3, g2)):
        tmp[pl.ds(8 * (x ^ j), 8)] = got[...].reshape(8, BX, BY)
    ratio_core(lambda c: tmp[:, c, :].reshape(256, BY), kf, kb, obs, out, (s0, s1, s3, s2))


SHARD, NOTED = sds(512, BY), sds(520, BY)
EDGE = sds(8, RIM, BY)
PACK = sds(4, BY, BY)
WHOLE = pltpu.VMEM((Z, BX, BY), F32)


def shard_cols_kernel(own, above, below, out):
    planes = [jnp.concatenate([above[k], own[k * BX : (k + 1) * BX], below[k]], axis=0)
              for k in range(8)]
    col_rims(planes, out)


def spread_kernel(picks, own, above, below, packs, *refs):
    count = len(picks)
    mats, outs, mid = refs[: 3 * count], refs[3 * count : -1], refs[-1]
    tiles = [jnp.concatenate([above[k], own[k * BX : (k + 1) * BX], below[k]], axis=0)
             for k in range(8)]
    tiles += [packs[k] for k in range(4)]
    for g in range(6):
        hi, lo = split(jnp.concatenate(tiles[2 * g : 2 * g + 2], axis=1))
        both = jnp.concatenate([hi, lo], axis=0)
        for n in range(count):
            o = dot(mats[3 * n][picks[n]], both)
            o = o[:BX] + o[BX:]
            mid[n, 2 * g] = o[:, :BY]
            mid[n, 2 * g + 1] = o[:, BY:]
    for n in range(count):
        out = outs[n]

        def put(k, v, out=out):
            out[k * BX : (k + 1) * BX] = v

        y_filter(mats[3 * n + 1].at[picks[n]], mats[3 * n + 2].at[picks[n]],
                 [mid[n, k] for k in range(8)], [mid[n, 8 + k] for k in range(4)], put)


def spread(picks, new, got, packs, mats, **more):
    return call(functools.partial(spread_kernel, picks), [SHARD] * len(picks),
                new, *got, packs, *mats, **more,
                scratch=[pltpu.VMEM((len(picks), 12, BX, BY), F32)])


def collect_columns(r, w, rims, put):
    for g in range(2):
        planes = [r[(4 * g + q) * BX : (4 * g + q + 1) * BX] for q in range(4)]
        hi, lo = split(jnp.concatenate(planes, axis=0))
        o = dot_turned(hi, w[:, :BY]) + dot_turned(hi, w[:, BY:]) + dot_turned(lo, w[:, :BY])
        for q in range(4):
            put(4 * g + q, o[q * BX : (q + 1) * BX])
        pairs = [jnp.concatenate(planes[2 * i : 2 * i + 2], axis=1) for i in range(2)]
        hi, lo = split(jnp.concatenate(pairs, axis=0))
        e = dot_turned(hi, rims[0]) + dot_turned(hi, rims[1]) + dot_turned(lo, rims[0])
        for i in range(2):
            put(8 + 2 * g + i, e[i * BX : (i + 1) * BX])


def collect_first_kernel(r0, r1, r3, wy, wr, mid):
    for j, r in enumerate((r0, r1, r3)):
        def put(k, v, j=j):
            mid[k, j * BX : (j + 1) * BX] = v

        collect_columns(r, wy.at[j], wr.at[j], put)


def collect_kernel(part, r2, wy, wr, lt, main, packs, late):
    def put_late(k, v):
        late[k] = v

    collect_columns(r2, wy.at[0], wr.at[0], put_late)
    for g in range(6):
        both = [jnp.concatenate([part[k], late[k]], axis=0) for k in (2 * g, 2 * g + 1)]
        hi, lo = split(jnp.concatenate(both, axis=1))
        o = dot(lt[0], hi) + dot(lt[0], lo) + dot(lt[1], hi)
        for i in range(2):
            k = 2 * g + i
            v = o[:, i * BY : (i + 1) * BY]
            if k < 8:
                main[k] = v
            else:
                packs[k - 8] = v


def add_cols_kernel(main, packs, own, up, down):
    near = lanes((BY, BY)) < BY // 2
    for k in range(8):
        pack = packs[k // 2]
        side = pltpu.roll(pack, BY // 2, 1) if k % 2 else pack
        v = main[k] + jnp.where(near, side, 0.0)
        up[k] = v[:RIM]
        own[k * BX : (k + 1) * BX] = v[RIM : RIM + BX]
        down[k] = v[RIM + BX :]


def add_rows_kernel(own, above, below, *refs):
    out, notes = refs[-1], refs[:-1]
    for k in range(8):
        r = k * BX
        out[r : r + RIM] = own[r : r + RIM] + above[k]
        out[r + RIM : r + BX] = own[r + RIM : r + BX] + below[k]
    for j, note in enumerate(notes):
        out[512 + 8 * j : 520 + 8 * j] = note[...] if j == 0 else note[512:]


def touch_kernel(out):
    out[...] = jnp.zeros_like(out)


def update_kernel(first, *refs):
    if first:
        f, mine, other, out, weight, top, bottom, turned = refs
    else:
        f, mine, other, weight, out = refs
    x = lax.axis_index("view") // 2
    if first:
        every = jnp.concatenate(
            [mine[512:], other[512:], jnp.zeros((64, 128), F32)], axis=0)
        turned[...] = jnp.transpose(every)
        outer = []
        for v in range(8):
            outer.append(turned[:BX, 8 * v + 4 : 8 * v + 5] * every[8 * v + 5 : 8 * v + 6])
        late = x >= 2
        for k in range(8):
            z_row = turned[pl.ds(pl.multiple_of(64 * (x % 2) + 8 * k, 8), 1), :]
            total = None
            for v in range(8):
                c = 8 * v + 6
                term = jnp.where(late, z_row[:, c + 1 : c + 2], z_row[:, c : c + 1]) * outer[v]
                total = term if total is None else total + term
            weight[k * BX : (k + 1) * BX] = total
        old = f[pl.ds(8 * x, 8)].reshape(512, BY)
    else:
        old = f[...]
    new = old * (mine[:512] + other[:512]) / weight[...]
    out[...] = new
    if first:
        for k in range(8):
            top[k] = new[k * BX : k * BX + RIM]
            bottom[k] = new[(k + 1) * BX - RIM : (k + 1) * BX]


def gather_kernel(own, one, three, two, f):
    x = lax.axis_index("view") // 2
    for j, ref in zip(ORDER, (own, one, three, two)):
        f[pl.ds(8 * (x ^ j), 8)] = ref[...].reshape(8, BX, BY)


def cols_kernel(offs, obs, packs, out, top, bottom):
    shift = offs[0, 1] + RIM
    outside = lanes((BX, BY)) + shift >= BY
    for k in range(Z):
        own = pltpu.roll(obs[k], BY - shift, 1)
        side = pltpu.roll(packs[k // 2], lax.rem(2 * BY - shift - BY // 2 * (k % 2), BY), 1)
        v = jnp.where(outside, side, own)
        out[k] = v
        top[k] = v[:SHIFT]
        bottom[k] = v[BX - SHIFT :]


def rows_kernel(offs, obs, above, below, out):
    ox = offs[0, 0]
    total = BX + 2 * SHIFT
    amount = lax.rem(2 * total - SHIFT - ox, total)
    for k in range(Z):
        wide = jnp.concatenate([above[k], obs[k], below[k]], axis=0)
        out[k] = pltpu.roll(wide, amount, 0)[:BX]


def along_rows(x, by):
    return lax.ppermute(x, "blk", [(i, (i + 4 * by) % 32) for i in range(32)])


def along_cols(x, by):
    return lax.ppermute(x, "blk", [(i, i // 4 * 4 + (i + by) % 4) for i in range(32)])


def view_swap(x, mask):
    return lax.ppermute(x, "view", [(i, i ^ mask) for i in range(8)])


def send_rows(top, bottom):
    return along_rows(bottom, 1), along_rows(top, -1)


def trade(*parts):
    return [p if j == 0 else view_swap(p, 2 * j) for j, p in zip(ORDER, parts)]


def local(estimate, observed, kernels, offsets):
    f = estimate[0]
    seen = observed[0, 0]
    packs = call(functools.partial(col_rims_kernel, 1), COLS, f)
    cols_b = along_cols(packs, -1)
    edges = call(functools.partial(row_rims_kernel, 0), ROWS, f, before=(packs,))
    rows_a = send_rows(*edges)
    lxf, wyf, wrf, kzf, kzb, note = own_matrices(offsets, kernels, before=edges[:1])
    obs_packs = call(obs_cols_kernel, [sds(Z // 2, BX, BY)], seen, before=edges[:1])
    obs_cols = along_cols(obs_packs, -1)
    obs, top, bottom = call(
        cols_kernel, [sds(Z, BX, BY), sds(Z, SHIFT, BY), sds(Z, SHIFT, BY)],
        offsets, seen, obs_cols, smem=(0,))
    above, below = send_rows(top, bottom)
    xa, packs = x_first((f,), 0, rows_a, lxf, before=(obs,))
    cols_a = along_cols(packs, -1)
    yb, *rims = y_first((f,), 1, cols_b, wyf, wrf, before=(xa,))
    rows_b = send_rows(*rims)
    obs = call(rows_kernel, [sds(Z, BX, BY)], offsets, obs, above, below, smem=(0,),
               before=(yb,))
    ga = call(second_y_kernel, [HALF], xa, cols_a, wyf, wrf, before=(obs,))
    gb = call(second_x_kernel, [HALF], yb, *rows_b, lxf, before=(ga,))
    parts = call(ratio_start_kernel, [SHARD] + [NOTED] * 3, ga, gb, kzf, kzb, obs, note,
                 scratch=[WHOLE])
    for step in range(ITERS):
        first = step == 0
        if not first:
            got = send_rows(top, bottom)
            packs = along_cols(call(shard_cols_kernel, [PACK], new, *got), -1)
            one, three = spread((1, 2), new, got, packs, [*near[:3], *near[:3]])
            two, own = spread((0, 0), new, got, packs, [*far[:3], *near[:3]], after=(one,))
            own, one, three, two = trade(own, one, three, two)
            mark = call(touch_kernel, [sds(8, BY)], before=(one, three))
            parts = call(ratio_kernel, [SHARD] * 4, one, three, two, own, kzf, kzb, obs,
                         before=(mark,), scratch=[WHOLE, WHOLE])
        own, one, three, two = trade(*parts)
        if first:
            near = call(near_matrices_kernel, many(3), note, one, three, scratch=TAP_SCRATCH)
            far = call(far_matrices_kernel, many(1), two, near[3], scratch=TAP_SCRATCH)
            notes = (note, one, three, two)
        part = call(collect_first_kernel, [sds(12, 192, BY)], own, one, three, *near[1:3])
        main, packs = call(collect_kernel, [sds(8, BY, BY), PACK], part, two, *far[1:],
                           scratch=[pltpu.VMEM((12, BX, BY), F32)])
        own, up, down = call(add_cols_kernel, [sds(512, BY), EDGE, EDGE],
                             main, along_cols(packs, 1))
        extra = notes if first else ()
        mine = call(add_rows_kernel, [sds(512 + 8 * len(extra), BY)],
                    own, *send_rows(up, down), *extra)
        other = view_swap(mine, 1)
        if first:
            new, weight, top, bottom = call(
                functools.partial(update_kernel, True),
                [sds(512, BY), sds(512, BY), EDGE, EDGE],
                f, mine, other, scratch=[pltpu.VMEM((128, 128), F32)])
        else:
            new = call(functools.partial(update_kernel, False), [sds(512, BY)],
                       new, mine, other, weight)
    return call(gather_kernel, [sds(Z, BX, BY)], *trade(new, new, new, new))[None]


def solution(mesh):
    in_specs = (
        P("blk", None, None, None),
        P("view", "blk", None, None, None),
        P("view", None, None),
        P("view", None),
    )
    out_specs = P("blk", None, None, None)
    return jax.shard_map(local, mesh=mesh, in_specs=in_specs, out_specs=out_specs, check_vma=False)
```

```python
import functools
import jax
import jax.numpy as jnp
from jax import lax
from jax.experimental import pallas as pl
from jax.experimental.pallas import tpu as pltpu
from jax.sharding import PartitionSpec as P

TAPS = 63
ITERS = 2
Z, BX, BY = 32, 64, 128
HALF_Z = Z // 2
RIM = 32
SHIFT = 16
GRID = 512
F32, BF16 = jnp.float32, jnp.bfloat16
PROF = 8


def split(x):
    hi = x.astype(BF16)
    return hi, (x - hi.astype(F32)).astype(BF16)


def dot(a, b):
    return jnp.dot(a, b, preferred_element_type=F32)


def wrap_of(pos):
    return jnp.where(pos >= GRID, 1, 0) - jnp.where(pos < 0, 1, 0)


def sds(*shape, dtype=F32):
    return jax.ShapeDtypeStruct(shape, dtype)


def call(body, out_shape, *args, smem=(), before=(), after=(), scratch=(), flops=1_000_000):
    specs = [
        pl.BlockSpec(memory_space=pltpu.SMEM if i in smem else pltpu.VMEM)
        for i in range(len(args))
    ]
    count, lead, tail = len(args), len(before), len(after)

    def inner(*refs):
        body(*refs[lead : lead + count], *refs[lead + count + tail :])

    loose = pl.BlockSpec(memory_space=pl.ANY)
    specs = [loose] * lead + specs + [loose] * tail
    size = sum(v.size * v.dtype.itemsize for v in (*args, *out_shape))
    outs = pl.pallas_call(
        inner,
        out_shape=out_shape,
        in_specs=specs,
        out_specs=[pl.BlockSpec(memory_space=pltpu.VMEM) for _ in out_shape],
        scratch_shapes=list(scratch),
        compiler_params=pltpu.CompilerParams(vmem_limit_bytes=40 * 1024 * 1024),
        cost_estimate=pl.CostEstimate(flops=flops, bytes_accessed=size, transcendentals=0),
    )(*before, *args, *after)
    return outs if len(outs) > 1 else outs[0]


def even_column():
    return lax.axis_index("blk") % 2 == 0


def partners():
    core = lax.axis_index("blk") % 2
    return 0, 1 + 2 * core, 3 - 2 * core, 2


def lanes(shape):
    return lax.broadcasted_iota(jnp.int32, shape, len(shape) - 1)


def rows_of(shape):
    return lax.broadcasted_iota(jnp.int32, shape, len(shape) - 2)


def tap_rows(taps, full, rows, depth=True):
    full[...] = jnp.zeros_like(full)
    full[:3, :TAPS] = taps
    x = full[...]
    hi, lo = split(x)
    mid, low = split(x - hi.astype(F32))
    parts = jnp.concatenate([hi, mid, low, jnp.zeros_like(hi)], axis=0)

    def moved(step, flip, width):
        j = lax.broadcasted_iota(jnp.int32, (BY, width), 0)
        target = (TAPS - 1 - j if flip else j) * step
        hot = jnp.where((lanes((BY, width)) == target) & (j < TAPS), 1.0, 0.0).astype(BF16)
        out = dot(parts, hot)
        return out[:8] + (out[8:16] + out[16:24])

    rows[...] = jnp.zeros_like(rows)
    flipped = moved(1, True, BY)
    rows[0:1, :BY] = x[0:1]
    rows[1:2, :BY] = flipped[0:1]
    rows[2:3, :BY] = x[1:2]
    rows[3:4, :BY] = flipped[1:2]
    if depth:
        rows[4:5, :512] = moved(8, False, 512)[2:3]
        rows[5:6, :512] = moved(8, True, 512)[2:3]


def block_start():
    block = lax.axis_index("blk")
    return (block // 4) * BX, (block % 4) * BY


def x_band(rows, row, s, ox, adjoint=False):
    base = jnp.broadcast_to(rows[row : row + 1, :BY], (BX, BY))
    band = pltpu.roll(base, 1, 1, stride=1, stride_axis=0)
    m = s + lanes((BX, BY)) - RIM
    i = s + ox + rows_of((BX, BY))
    keep = (wrap_of(m + ox) == 0) if adjoint else (wrap_of(i) == wrap_of(m))
    return jnp.where(keep, band, 0.0)


def x_band_turned(rows, row, s, ox):
    base = jnp.broadcast_to(rows[row : row + 1, :256], (BY, 256))
    band = pltpu.roll(base, 193, 1, stride=1, stride_axis=0)[:, :BY]
    m = s + rows_of((BY, BY)) - RIM
    i = s + ox + lanes((BY, BY))
    keep = (wrap_of(i) == wrap_of(m)) & (lanes((BY, BY)) < BX)
    return jnp.where(keep, band, 0.0)[:, :BX]


def y_toeplitz(rows, row):
    base = jnp.broadcast_to(rows[row : row + 1, :256], (BY + 2 * RIM, 256))
    return pltpu.roll(base, 193, 1, stride=1, stride_axis=0)[:, :BY]


def y_band(rows, row, cs, oy):
    band = y_toeplitz(rows, row)
    m = cs + rows_of(band.shape)
    j = cs + oy + RIM + lanes(band.shape)
    return jnp.where(wrap_of(j) == wrap_of(m), band, 0.0)


def y_profile(rows, row, cs, oy):
    band = y_toeplitz(rows, row)
    m = cs + rows_of(band.shape) - RIM
    return jnp.sum(jnp.where(wrap_of(m + oy) == 0, band, 0.0), axis=0, keepdims=True)


def z_band(rows, row, shift):
    amount = lax.rem(1024 - 248 - 8 * shift, 1024)
    moved = pltpu.roll(rows[...], amount, 1)[row : row + 1]
    base = jnp.broadcast_to(moved, (256, 1024))
    return pltpu.roll(base, 0, 1, stride=1, stride_axis=0)[:, :256]


def put_x(ref, band):
    hi, lo = split(band)
    top = jnp.concatenate([hi, hi], axis=1)
    bottom = jnp.concatenate([lo, jnp.zeros_like(lo)], axis=1)
    ref[...] = jnp.concatenate([top, bottom], axis=0)


def put_y(main, rims, band):
    hi, lo = split(band[:BY])
    main[...] = jnp.concatenate([hi, lo], axis=1)
    side = band[BY:]
    none = jnp.zeros_like(side)
    whole = jnp.concatenate([jnp.concatenate([side, none], axis=1),
                             jnp.concatenate([none, side], axis=1)], axis=0)
    rims[0], rims[1] = split(whole)


def own_kernel(offs, taps, lxf, wyf, wrf, kzf, kzb, note, full, rows):
    tap_rows(taps[0], full, rows)
    s, cs = block_start()
    ox, oy, oz = offs[0, 0], offs[0, 1], offs[0, 2]
    put_x(lxf, x_band(rows, 1, s, ox))
    put_y(wyf, wrf, y_band(rows, 2, cs, oy))
    front_z = z_band(rows, 5, oz)
    kzf[0], kzf[1] = split(front_z)
    kzb[0], kzb[1] = split(z_band(rows, 4, -oz))
    back_x = x_band(rows, 0, s, ox, True)
    turned = jnp.transpose(jnp.concatenate([back_x, jnp.zeros_like(back_x)], axis=0))
    prof_x = jnp.sum(turned, axis=0, keepdims=True)
    prof_y = y_profile(rows, 3, cs, oy)
    prof_z = jnp.sum(front_z, axis=0, keepdims=True)
    lane = lanes((1, BY))
    shifts = jnp.where(lane == 0, ox, jnp.where(lane == 1, oy, 0)).astype(F32)
    note[...] = jnp.concatenate(
        [full[:3], shifts, prof_x, prof_y, prof_z[:, :128], prof_z[:, 128:]], axis=0)


LX, WY = sds(128, 256, dtype=BF16), sds(128, 256, dtype=BF16)
WR, KZ = sds(2, 128, 256, dtype=BF16), sds(2, 256, 256, dtype=BF16)
LT = sds(2, 128, 256, dtype=BF16)
TAP_SCRATCH = [pltpu.VMEM((8, BY), F32), pltpu.VMEM((8, 1024), F32)]


def own_matrices(offs, taps, **more):
    return call(own_kernel, [LX, WY, WR, KZ, KZ, sds(PROF, 128)], offs, taps, smem=(0,),
                scratch=TAP_SCRATCH, **more)


def view_matrices(note, lx, wy, wr, lt, j, full, rows):
    s, cs = block_start()
    tap_rows(note[:3, :TAPS], full, rows, False)
    shifts = note[3:4]
    ox = shifts[:, 0:1].astype(jnp.int32)
    oy = shifts[:, 1:2].astype(jnp.int32)
    put_x(lx, x_band(rows, 1, s, ox))
    put_y(wy, wr, y_band(rows, 2, cs, oy))
    hi, lo = split(x_band_turned(rows, 0, s, ox))
    lt[0, :, j * BX : (j + 1) * BX] = hi
    lt[1, :, j * BX : (j + 1) * BX] = lo


def near_matrices_kernel(note, m1, m3, lx, wy, wr, lt, full, rows):
    lt[...] = jnp.zeros_like(lt)
    for j, ref in enumerate((note, m1, m3)):
        one = ref[...] if j == 0 else ref[512:]
        view_matrices(one, lx.at[j], wy.at[j], wr.at[j], lt, j, full, rows)


def far_matrices_kernel(m2, old, lx, wy, wr, lt, full, rows):
    lt[...] = old[...]
    view_matrices(m2[512:], lx.at[0], wy.at[0], wr.at[0], lt, 3, full, rows)


def many(count):
    return [sds(count, *v.shape, dtype=v.dtype) for v in (LX, WY, WR)] + [LT]


def row_rims(planes, top, bottom):
    for k, plane in enumerate(planes):
        top[k] = plane[:RIM]
        bottom[k] = plane[BX - RIM :]


def col_rims(planes, out):
    there = lanes(planes[0].shape) >= BY // 2
    for g in range(len(planes) // 2):
        out[g] = jnp.where(there, pltpu.roll(planes[2 * g + 1], BY // 2, 1), planes[2 * g])


ROWS = [sds(HALF_Z, RIM, BY), sds(HALF_Z, RIM, BY)]
COLS = [sds(HALF_Z // 2, BX, BY)]
HALF = sds(HALF_Z, BX, BY)


def planes_of(*refs, half=None):
    planes = []
    for ref in refs:
        if len(ref.shape) == 3:
            skip = 0 if half is None else half * HALF_Z
            stop = ref.shape[0] if half is None else skip + HALF_Z
            planes += [ref[k] for k in range(skip, stop)]
        else:
            planes += [ref[k * BX : (k + 1) * BX] for k in range(ref.shape[0] // BX)]
    return planes


def row_rims_kernel(half, *refs):
    row_rims(planes_of(*refs[:-2], half=half), *refs[-2:])


def col_rims_kernel(half, *refs):
    col_rims(planes_of(*refs[:-1], half=half), refs[-1])


def obs_cols_kernel(obs, out):
    col_rims(planes_of(obs), out)


def x_filter(mat, own, above, below, put):
    for g in range(HALF_Z // 2):
        both = []
        for k in (2 * g, 2 * g + 1):
            both.append(jnp.concatenate([above[k], own[k], below[k]], axis=0))
        o = x_pair(mat, jnp.concatenate(both, axis=1))
        put(2 * g, o[:, :BY])
        put(2 * g + 1, o[:, BY:])


def x_pair(mat, wide):
    hi, lo = split(wide)
    o = dot(mat[...], jnp.concatenate([hi, lo], axis=0))
    return o[:BX] + o[BX:]


def y_filter(main, rims, own, packs, put):
    for g in range(len(own) // 4):
        x = jnp.concatenate([own[4 * g + q] for q in range(4)], axis=0)
        hi, lo = split(x)
        o = dot(hi, main[...])
        o = o[:, :BY] + o[:, BY:] + dot(lo, main[:, :BY])
        hi, lo = split(jnp.concatenate([packs[2 * g], packs[2 * g + 1]], axis=0))
        r = dot(hi, rims[0]) + dot(hi, rims[1]) + dot(lo, rims[0])
        for q in range(4):
            i = q // 2 * BX
            j = q % 2 * BY
            put(4 * g + q, o[q * BX : (q + 1) * BX] + r[i : i + BX, j : j + BY])


def dot_turned(a, b):
    return lax.dot_general(a, b, (((1,), (1,)), ((), ())), preferred_element_type=F32)


def z_filter(mat, tiles):
    hi, lo = split(tiles)
    return dot(mat[0], hi) + dot(mat[0], lo) + dot(mat[1], hi)


def storer(ref, place=lambda k: k):
    def put(k, v):
        ref[place(k)] = v

    return put


def y_first_kernel(count, half, *refs):
    src, (packs, wy, wr, yb, top, bottom) = refs[:count], refs[count:]

    def put(k, v):
        yb[k] = v
        top[k] = v[:RIM]
        bottom[k] = v[BX - RIM :]

    y_filter(wy, wr, planes_of(*src, half=half), packs, put)


def x_first_kernel(count, half, *refs):
    src, (above, below, lx, xa, packs) = refs[:count], refs[count:]
    x_filter(lx, planes_of(*src, half=half), above, below, storer(xa))
    col_rims(planes_of(xa), packs)


def y_first(src, half, cols, wy, wr, **more):
    return call(functools.partial(y_first_kernel, len(src), half), [HALF, *ROWS],
                *src, cols, wy, wr, **more)


def x_first(src, half, rows, lx, **more):
    return call(functools.partial(x_first_kernel, len(src), half), [HALF, *COLS],
                *src, *rows, lx, **more)


def ratio_core(load, kf, kb, obs, out, sends):
    for t in range(BX // 16):
        cut = [slice(16 * t, 16 * t + 8), slice(16 * t + 8, 16 * t + 16)]
        blurred = z_filter(kf, jnp.concatenate([load(c) for c in cut], axis=1))
        seen = jnp.concatenate([obs[:, c, :].reshape(256, BY) for c in cut], axis=1)
        back = z_filter(kb, seen / blurred)
        for i, c in enumerate(cut):
            out[:, c, :] = back[:, i * BY : (i + 1) * BY].reshape(Z, 8, BY)
    x = lax.axis_index("view") // 2
    for j, send in zip(partners(), sends):
        send[:512] = out[pl.ds(8 * (x ^ j), 8)].reshape(512, BY)


def second_x_kernel(yb, above, below, lx, out):
    x_filter(lx, planes_of(yb), above, below, storer(out))


def second_y_kernel(xa, packs, wy, wr, out):
    y_filter(wy, wr, planes_of(xa), packs, storer(out))


def ratio_start_kernel(ga, gb, kf, kb, obs, note, s0, s1, s3, s2, out):
    def load(c):
        return jnp.concatenate([ga[:, c, :], gb[:, c, :]], axis=0).reshape(256, BY)

    ratio_core(load, kf, kb, obs, out, (s0, s1, s3, s2))
    for send in (s1, s3, s2):
        send[512:] = note[...]


def ratio_kernel(g1, g3, g2, g0, kf, kb, obs, s0, s1, s3, s2, tmp, out):
    x = lax.axis_index("view") // 2
    for j, got in zip(partners(), (g0, g1, g3, g2)):
        tmp[pl.ds(8 * (x ^ j), 8)] = got[...].reshape(8, BX, BY)
    ratio_core(lambda c: tmp[:, c, :].reshape(256, BY), kf, kb, obs, out, (s0, s1, s3, s2))


SHARD, NOTED = sds(512, BY), sds(520, BY)
EDGE = sds(8, RIM, BY)
PACK = sds(4, BY, BY)
WHOLE = pltpu.VMEM((Z, BX, BY), F32)


def shard_cols_kernel(own, above, below, out):
    planes = [jnp.concatenate([above[k], own[k * BX : (k + 1) * BX], below[k]], axis=0)
              for k in range(8)]
    col_rims(planes, out)


def spread_kernel(picks, own, above, below, packs, *refs):
    count = len(picks)
    mats, outs, mid = refs[: 3 * count], refs[3 * count : -1], refs[-1]
    tiles = [jnp.concatenate([above[k], own[k * BX : (k + 1) * BX], below[k]], axis=0)
             for k in range(8)]
    tiles += [packs[k] for k in range(4)]
    for g in range(6):
        hi, lo = split(jnp.concatenate(tiles[2 * g : 2 * g + 2], axis=1))
        both = jnp.concatenate([hi, lo], axis=0)
        for n in range(count):
            o = dot(mats[3 * n][picks[n]], both)
            o = o[:BX] + o[BX:]
            mid[n, 2 * g] = o[:, :BY]
            mid[n, 2 * g + 1] = o[:, BY:]
    for n in range(count):
        out = outs[n]

        def put(k, v, out=out):
            out[k * BX : (k + 1) * BX] = v

        y_filter(mats[3 * n + 1].at[picks[n]], mats[3 * n + 2].at[picks[n]],
                 [mid[n, k] for k in range(8)], [mid[n, 8 + k] for k in range(4)], put)


def spread(picks, new, got, packs, mats, **more):
    return call(functools.partial(spread_kernel, picks), [SHARD] * len(picks),
                new, *got, packs, *mats, **more,
                scratch=[pltpu.VMEM((len(picks), 12, BX, BY), F32)])


def collect_columns(r, w, rims, put):
    for g in range(2):
        planes = [r[(4 * g + q) * BX : (4 * g + q + 1) * BX] for q in range(4)]
        hi, lo = split(jnp.concatenate(planes, axis=0))
        o = dot_turned(hi, w[:, :BY]) + dot_turned(hi, w[:, BY:]) + dot_turned(lo, w[:, :BY])
        for q in range(4):
            put(4 * g + q, o[q * BX : (q + 1) * BX])
        pairs = [jnp.concatenate(planes[2 * i : 2 * i + 2], axis=1) for i in range(2)]
        hi, lo = split(jnp.concatenate(pairs, axis=0))
        e = dot_turned(hi, rims[0]) + dot_turned(hi, rims[1]) + dot_turned(lo, rims[0])
        for i in range(2):
            put(8 + 2 * g + i, e[i * BX : (i + 1) * BX])


def collect_first_kernel(r0, r1, r3, wy, wr, mid):
    for j, r in enumerate((r0, r1, r3)):
        def put(k, v, j=j):
            mid[k, j * BX : (j + 1) * BX] = v

        collect_columns(r, wy.at[j], wr.at[j], put)


def collect_kernel(part, r2, wy, wr, lt, main, packs, late):
    def put_late(k, v):
        late[k] = v

    collect_columns(r2, wy.at[0], wr.at[0], put_late)
    for g in range(6):
        both = [jnp.concatenate([part[k], late[k]], axis=0) for k in (2 * g, 2 * g + 1)]
        hi, lo = split(jnp.concatenate(both, axis=1))
        o = dot(lt[0], hi) + dot(lt[0], lo) + dot(lt[1], hi)
        for i in range(2):
            k = 2 * g + i
            v = o[:, i * BY : (i + 1) * BY]
            if k < 8:
                main[k] = v
            else:
                packs[k - 8] = v


def add_cols_kernel(main, packs, own, up, down):
    near = lanes((BY, BY)) < BY // 2
    for k in range(8):
        pack = packs[k // 2]
        side = pltpu.roll(pack, BY // 2, 1) if k % 2 else pack
        v = main[k] + jnp.where(near, side, 0.0)
        up[k] = v[:RIM]
        own[k * BX : (k + 1) * BX] = v[RIM : RIM + BX]
        down[k] = v[RIM + BX :]


def add_rows_kernel(own, above, below, *refs):
    out, notes = refs[-1], refs[:-1]
    for k in range(8):
        r = k * BX
        out[r : r + RIM] = own[r : r + RIM] + above[k]
        out[r + RIM : r + BX] = own[r + RIM : r + BX] + below[k]
    for j, note in enumerate(notes):
        out[512 + 8 * j : 520 + 8 * j] = note[...] if j == 0 else note[512:]


def touch_kernel(out):
    out[...] = jnp.zeros_like(out)


def update_kernel(first, *refs):
    if first:
        f, mine, other, out, weight, top, bottom, turned = refs
    else:
        f, mine, other, weight, out = refs
    x = lax.axis_index("view") // 2
    if first:
        every = jnp.concatenate(
            [mine[512:], other[512:], jnp.zeros((64, 128), F32)], axis=0)
        turned[...] = jnp.transpose(every)
        outer = []
        for v in range(8):
            outer.append(turned[:BX, 8 * v + 4 : 8 * v + 5] * every[8 * v + 5 : 8 * v + 6])
        late = x >= 2
        for k in range(8):
            z_row = turned[pl.ds(pl.multiple_of(64 * (x % 2) + 8 * k, 8), 1), :]
            total = None
            for v in range(8):
                c = 8 * v + 6
                term = jnp.where(late, z_row[:, c + 1 : c + 2], z_row[:, c : c + 1]) * outer[v]
                total = term if total is None else total + term
            weight[k * BX : (k + 1) * BX] = total
        old = f[pl.ds(8 * x, 8)].reshape(512, BY)
    else:
        old = f[...]
    new = old * (mine[:512] + other[:512]) / weight[...]
    out[...] = new
    if first:
        for k in range(8):
            top[k] = new[k * BX : k * BX + RIM]
            bottom[k] = new[(k + 1) * BX - RIM : (k + 1) * BX]


def gather_kernel(own, one, three, two, f):
    x = lax.axis_index("view") // 2
    for j, ref in zip(partners(), (own, one, three, two)):
        f[pl.ds(8 * (x ^ j), 8)] = ref[...].reshape(8, BX, BY)


def cols_kernel(offs, obs, packs, out, top, bottom):
    shift = offs[0, 1] + RIM
    outside = lanes((BX, BY)) + shift >= BY
    for k in range(Z):
        own = pltpu.roll(obs[k], BY - shift, 1)
        side = pltpu.roll(packs[k // 2], lax.rem(2 * BY - shift - BY // 2 * (k % 2), BY), 1)
        v = jnp.where(outside, side, own)
        out[k] = v
        top[k] = v[:SHIFT]
        bottom[k] = v[BX - SHIFT :]


def rows_kernel(offs, obs, above, below, out):
    ox = offs[0, 0]
    total = BX + 2 * SHIFT
    amount = lax.rem(2 * total - SHIFT - ox, total)
    for k in range(Z):
        wide = jnp.concatenate([above[k], obs[k], below[k]], axis=0)
        out[k] = pltpu.roll(wide, amount, 0)[:BX]


def along_rows(x, by):
    return lax.ppermute(x, "blk", [(i, (i + 4 * by) % 32) for i in range(32)])


def along_cols(x, by):
    return lax.ppermute(x, "blk", [(i, i // 4 * 4 + (i + by) % 4) for i in range(32)])


def view_swap(x, mask):
    return lax.ppermute(x, "view", [(i, i ^ mask) for i in range(8)])


def send_rows(top, bottom):
    return along_rows(bottom, 1), along_rows(top, -1)


def trade(own, one, three, two):
    def swap(x, even, odd):
        pairs = [(v * 32 + b, (v ^ (2 * (odd if b % 2 else even))) * 32 + b)
                 for v in range(8) for b in range(32)]
        return lax.ppermute(x, ("view", "blk"), pairs)

    return own, swap(one, 1, 3), swap(three, 3, 1), swap(two, 2, 2)


def local(estimate, observed, kernels, offsets):
    f = estimate[0]
    seen = observed[0, 0]
    packs = call(functools.partial(col_rims_kernel, 1), COLS, f)
    cols_b = along_cols(packs, -1)
    edges = call(functools.partial(row_rims_kernel, 0), ROWS, f, before=(packs,))
    rows_a = send_rows(*edges)
    lxf, wyf, wrf, kzf, kzb, note = own_matrices(offsets, kernels, before=edges[:1])
    obs_packs = call(obs_cols_kernel, [sds(Z // 2, BX, BY)], seen, before=edges[:1])
    obs_cols = along_cols(obs_packs, -1)
    obs, top, bottom = call(
        cols_kernel, [sds(Z, BX, BY), sds(Z, SHIFT, BY), sds(Z, SHIFT, BY)],
        offsets, seen, obs_cols, smem=(0,))
    above, below = send_rows(top, bottom)
    xa, packs = x_first((f,), 0, rows_a, lxf, before=(obs,))
    cols_a = along_cols(packs, -1)
    yb, *rims = y_first((f,), 1, cols_b, wyf, wrf, before=(xa,))
    rows_b = send_rows(*rims)
    obs = call(rows_kernel, [sds(Z, BX, BY)], offsets, obs, above, below, smem=(0,),
               before=(yb,))
    ga = call(second_y_kernel, [HALF], xa, cols_a, wyf, wrf, before=(obs,))
    gb = call(second_x_kernel, [HALF], yb, *rows_b, lxf, before=(ga,))
    parts = call(ratio_start_kernel, [SHARD] + [NOTED] * 3, ga, gb, kzf, kzb, obs, note,
                 scratch=[WHOLE])
    for step in range(ITERS):
        first = step == 0
        if not first:
            got = send_rows(top, bottom)
            packs = along_cols(call(shard_cols_kernel, [PACK], new, *got), -1)
            one, three = spread((1, 2), new, got, packs, [*near[:3], *near[:3]])
            two, own = spread((0, 0), new, got, packs, [*far[:3], *near[:3]], after=(one,))
            own, one, three, two = trade(own, one, three, two)
            mark = call(touch_kernel, [sds(8, BY)], before=(one, three))
            parts = call(ratio_kernel, [SHARD] * 4, one, three, two, own, kzf, kzb, obs,
                         before=(mark,), scratch=[WHOLE, WHOLE])
        own, one, three, two = trade(*parts)
        if first:
            near = call(near_matrices_kernel, many(3), note, one, three, scratch=TAP_SCRATCH)
            far = call(far_matrices_kernel, many(1), two, near[3], scratch=TAP_SCRATCH)
            notes = (note, one, three, two)
        part = call(collect_first_kernel, [sds(12, 192, BY)], own, one, three, *near[1:3])
        main, packs = call(collect_kernel, [sds(8, BY, BY), PACK], part, two, *far[1:],
                           scratch=[pltpu.VMEM((12, BX, BY), F32)])
        own, up, down = call(add_cols_kernel, [sds(512, BY), EDGE, EDGE],
                             main, along_cols(packs, 1))
        extra = notes if first else ()
        mine = call(add_rows_kernel, [sds(512 + 8 * len(extra), BY)],
                    own, *send_rows(up, down), *extra)
        other = view_swap(mine, 1)
        if first:
            new, weight, top, bottom = call(
                functools.partial(update_kernel, True),
                [sds(512, BY), sds(512, BY), EDGE, EDGE],
                f, mine, other, scratch=[pltpu.VMEM((128, 128), F32)])
        else:
            new = call(functools.partial(update_kernel, False), [sds(512, BY)],
                       new, mine, other, weight)
    return call(gather_kernel, [sds(Z, BX, BY)], *trade(new, new, new, new))[None]


def solution(mesh):
    in_specs = (
        P("blk", None, None, None),
        P("view", "blk", None, None, None),
        P("view", None, None),
        P("view", None),
    )
    out_specs = P("blk", None, None, None)
    return jax.shard_map(local, mesh=mesh, in_specs=in_specs, out_specs=out_specs, check_vma=False)
```

```python
import functools
import jax
import jax.numpy as jnp
from jax import lax
from jax.experimental import pallas as pl
from jax.experimental.pallas import tpu as pltpu
from jax.sharding import PartitionSpec as P

TAPS = 63
ITERS = 2
Z, BX, BY = 32, 64, 128
HALF_Z = Z // 2
RIM = 32
SHIFT = 16
GRID = 512
F32, BF16 = jnp.float32, jnp.bfloat16
PROF = 8


def split(x):
    hi = x.astype(BF16)
    return hi, (x - hi.astype(F32)).astype(BF16)


def dot(a, b):
    return jnp.dot(a, b, preferred_element_type=F32)


def wrap_of(pos):
    return jnp.where(pos >= GRID, 1, 0) - jnp.where(pos < 0, 1, 0)


def sds(*shape, dtype=F32):
    return jax.ShapeDtypeStruct(shape, dtype)


def call(body, out_shape, *args, smem=(), before=(), after=(), scratch=(), flops=1_000_000):
    specs = [
        pl.BlockSpec(memory_space=pltpu.SMEM if i in smem else pltpu.VMEM)
        for i in range(len(args))
    ]
    count, lead, tail = len(args), len(before), len(after)

    def inner(*refs):
        body(*refs[lead : lead + count], *refs[lead + count + tail :])

    loose = pl.BlockSpec(memory_space=pl.ANY)
    specs = [loose] * lead + specs + [loose] * tail
    size = sum(v.size * v.dtype.itemsize for v in (*args, *out_shape))
    outs = pl.pallas_call(
        inner,
        out_shape=out_shape,
        in_specs=specs,
        out_specs=[pl.BlockSpec(memory_space=pltpu.VMEM) for _ in out_shape],
        scratch_shapes=list(scratch),
        compiler_params=pltpu.CompilerParams(vmem_limit_bytes=40 * 1024 * 1024),
        cost_estimate=pl.CostEstimate(flops=flops, bytes_accessed=size, transcendentals=0),
    )(*before, *args, *after)
    return outs if len(outs) > 1 else outs[0]


def even_column():
    return lax.axis_index("blk") % 2 == 0


def partners():
    core = lax.axis_index("blk") % 2
    return 0, 1 + 2 * core, 3 - 2 * core, 2


def lanes(shape):
    return lax.broadcasted_iota(jnp.int32, shape, len(shape) - 1)


def rows_of(shape):
    return lax.broadcasted_iota(jnp.int32, shape, len(shape) - 2)


def tap_rows(taps, full, rows, depth=True):
    full[...] = jnp.zeros_like(full)
    full[:3, :TAPS] = taps
    x = full[...]
    hi, lo = split(x)
    mid, low = split(x - hi.astype(F32))
    parts = jnp.concatenate([hi, mid, low, jnp.zeros_like(hi)], axis=0)

    def moved(step, flip, width):
        j = lax.broadcasted_iota(jnp.int32, (BY, width), 0)
        target = (TAPS - 1 - j if flip else j) * step
        hot = jnp.where((lanes((BY, width)) == target) & (j < TAPS), 1.0, 0.0).astype(BF16)
        out = dot(parts, hot)
        return out[:8] + (out[8:16] + out[16:24])

    rows[...] = jnp.zeros_like(rows)
    flipped = moved(1, True, BY)
    rows[0:1, :BY] = x[0:1]
    rows[1:2, :BY] = flipped[0:1]
    rows[2:3, :BY] = x[1:2]
    rows[3:4, :BY] = flipped[1:2]
    if depth:
        rows[4:5, :512] = moved(8, False, 512)[2:3]
        rows[5:6, :512] = moved(8, True, 512)[2:3]


def block_start():
    block = lax.axis_index("blk")
    return (block // 4) * BX, (block % 4) * BY


def x_band(rows, row, s, ox, adjoint=False):
    base = jnp.broadcast_to(rows[row : row + 1, :BY], (BX, BY))
    band = pltpu.roll(base, 1, 1, stride=1, stride_axis=0)
    m = s + lanes((BX, BY)) - RIM
    i = s + ox + rows_of((BX, BY))
    keep = (wrap_of(m + ox) == 0) if adjoint else (wrap_of(i) == wrap_of(m))
    return jnp.where(keep, band, 0.0)


def x_band_turned(rows, row, s, ox):
    base = jnp.broadcast_to(rows[row : row + 1, :256], (BY, 256))
    band = pltpu.roll(base, 193, 1, stride=1, stride_axis=0)[:, :BY]
    m = s + rows_of((BY, BY)) - RIM
    i = s + ox + lanes((BY, BY))
    keep = (wrap_of(i) == wrap_of(m)) & (lanes((BY, BY)) < BX)
    return jnp.where(keep, band, 0.0)[:, :BX]


def y_toeplitz(rows, row):
    base = jnp.broadcast_to(rows[row : row + 1, :256], (BY + 2 * RIM, 256))
    return pltpu.roll(base, 193, 1, stride=1, stride_axis=0)[:, :BY]


def y_band(rows, row, cs, oy):
    band = y_toeplitz(rows, row)
    m = cs + rows_of(band.shape)
    j = cs + oy + RIM + lanes(band.shape)
    return jnp.where(wrap_of(j) == wrap_of(m), band, 0.0)


def y_profile(rows, row, cs, oy):
    band = y_toeplitz(rows, row)
    m = cs + rows_of(band.shape) - RIM
    return jnp.sum(jnp.where(wrap_of(m + oy) == 0, band, 0.0), axis=0, keepdims=True)


def z_band(rows, row, shift):
    amount = lax.rem(1024 - 248 - 8 * shift, 1024)
    moved = pltpu.roll(rows[...], amount, 1)[row : row + 1]
    base = jnp.broadcast_to(moved, (256, 1024))
    return pltpu.roll(base, 0, 1, stride=1, stride_axis=0)[:, :256]


def put_x(ref, band):
    hi, lo = split(band)
    top = jnp.concatenate([hi, hi], axis=1)
    bottom = jnp.concatenate([lo, jnp.zeros_like(lo)], axis=1)
    ref[...] = jnp.concatenate([top, bottom], axis=0)


def put_y(main, rims, band):
    hi, lo = split(band[:BY])
    main[...] = jnp.concatenate([hi, lo], axis=1)
    side = band[BY:]
    none = jnp.zeros_like(side)
    whole = jnp.concatenate([jnp.concatenate([side, none], axis=1),
                             jnp.concatenate([none, side], axis=1)], axis=0)
    rims[0], rims[1] = split(whole)


def own_kernel(offs, taps, lxf, wyf, wrf, kzf, kzb, note, full, rows):
    tap_rows(taps[0], full, rows)
    s, cs = block_start()
    ox, oy, oz = offs[0, 0], offs[0, 1], offs[0, 2]
    put_x(lxf, x_band(rows, 1, s, ox))
    put_y(wyf, wrf, y_band(rows, 2, cs, oy))
    front_z = z_band(rows, 5, oz)
    kzf[0], kzf[1] = split(front_z)
    kzb[0], kzb[1] = split(z_band(rows, 4, -oz))
    back_x = x_band(rows, 0, s, ox, True)
    turned = jnp.transpose(jnp.concatenate([back_x, jnp.zeros_like(back_x)], axis=0))
    prof_x = jnp.sum(turned, axis=0, keepdims=True)
    prof_y = y_profile(rows, 3, cs, oy)
    prof_z = jnp.sum(front_z, axis=0, keepdims=True)
    lane = lanes((1, BY))
    shifts = jnp.where(lane == 0, ox, jnp.where(lane == 1, oy, 0)).astype(F32)
    note[...] = jnp.concatenate(
        [full[:3], shifts, prof_x, prof_y, prof_z[:, :128], prof_z[:, 128:]], axis=0)


LX, WY = sds(128, 256, dtype=BF16), sds(128, 256, dtype=BF16)
WR, KZ = sds(2, 128, 256, dtype=BF16), sds(2, 256, 256, dtype=BF16)
LT = sds(2, 128, 256, dtype=BF16)
TAP_SCRATCH = [pltpu.VMEM((8, BY), F32), pltpu.VMEM((8, 1024), F32)]


def own_matrices(offs, taps, **more):
    return call(own_kernel, [LX, WY, WR, KZ, KZ, sds(PROF, 128)], offs, taps, smem=(0,),
                scratch=TAP_SCRATCH, **more)


def view_matrices(note, lx, wy, wr, lt, j, full, rows):
    s, cs = block_start()
    tap_rows(note[:3, :TAPS], full, rows, False)
    shifts = note[3:4]
    ox = shifts[:, 0:1].astype(jnp.int32)
    oy = shifts[:, 1:2].astype(jnp.int32)
    put_x(lx, x_band(rows, 1, s, ox))
    put_y(wy, wr, y_band(rows, 2, cs, oy))
    hi, lo = split(x_band_turned(rows, 0, s, ox))
    lt[0, :, j * BX : (j + 1) * BX] = hi
    lt[1, :, j * BX : (j + 1) * BX] = lo


def near_matrices_kernel(note, m1, m3, lx, wy, wr, lt, full, rows):
    lt[...] = jnp.zeros_like(lt)
    for j, ref in enumerate((note, m1, m3)):
        one = ref[...] if j == 0 else ref[512:]
        view_matrices(one, lx.at[j], wy.at[j], wr.at[j], lt, j, full, rows)


def far_matrices_kernel(m2, old, lx, wy, wr, lt, full, rows):
    lt[...] = old[...]
    view_matrices(m2[512:], lx.at[0], wy.at[0], wr.at[0], lt, 3, full, rows)


def many(count):
    return [sds(count, *v.shape, dtype=v.dtype) for v in (LX, WY, WR)] + [LT]


def row_rims(planes, top, bottom):
    for k, plane in enumerate(planes):
        top[k] = plane[:RIM]
        bottom[k] = plane[BX - RIM :]


def col_rims(planes, out):
    there = lanes(planes[0].shape) >= BY // 2
    for g in range(len(planes) // 2):
        out[g] = jnp.where(there, pltpu.roll(planes[2 * g + 1], BY // 2, 1), planes[2 * g])


ROWS = [sds(HALF_Z, RIM, BY), sds(HALF_Z, RIM, BY)]
COLS = [sds(HALF_Z // 2, BX, BY)]
HALF = sds(HALF_Z, BX, BY)


def planes_of(*refs, half=None):
    planes = []
    for ref in refs:
        if len(ref.shape) == 3:
            skip = 0 if half is None else half * HALF_Z
            stop = ref.shape[0] if half is None else skip + HALF_Z
            planes += [ref[k] for k in range(skip, stop)]
        else:
            planes += [ref[k * BX : (k + 1) * BX] for k in range(ref.shape[0] // BX)]
    return planes


def row_rims_kernel(half, *refs):
    row_rims(planes_of(*refs[:-2], half=half), *refs[-2:])


def col_rims_kernel(half, *refs):
    col_rims(planes_of(*refs[:-1], half=half), refs[-1])


def obs_cols_kernel(obs, out):
    col_rims(planes_of(obs), out)


def x_filter(mat, own, above, below, put):
    for g in range(HALF_Z // 2):
        both = []
        for k in (2 * g, 2 * g + 1):
            both.append(jnp.concatenate([above[k], own[k], below[k]], axis=0))
        o = x_pair(mat, jnp.concatenate(both, axis=1))
        put(2 * g, o[:, :BY])
        put(2 * g + 1, o[:, BY:])


def x_pair(mat, wide):
    hi, lo = split(wide)
    o = dot(mat[...], jnp.concatenate([hi, lo], axis=0))
    return o[:BX] + o[BX:]


def y_filter(main, rims, own, packs, put):
    for g in range(len(own) // 4):
        x = jnp.concatenate([own[4 * g + q] for q in range(4)], axis=0)
        hi, lo = split(x)
        o = dot(hi, main[...])
        o = o[:, :BY] + o[:, BY:] + dot(lo, main[:, :BY])
        hi, lo = split(jnp.concatenate([packs[2 * g], packs[2 * g + 1]], axis=0))
        r = dot(hi, rims[0]) + dot(hi, rims[1]) + dot(lo, rims[0])
        for q in range(4):
            i = q // 2 * BX
            j = q % 2 * BY
            put(4 * g + q, o[q * BX : (q + 1) * BX] + r[i : i + BX, j : j + BY])


def dot_turned(a, b):
    return lax.dot_general(a, b, (((1,), (1,)), ((), ())), preferred_element_type=F32)


def z_filter(mat, tiles):
    hi, lo = split(tiles)
    return dot(mat[0], hi) + dot(mat[0], lo) + dot(mat[1], hi)


def storer(ref, place=lambda k: k):
    def put(k, v):
        ref[place(k)] = v

    return put


def y_first_kernel(count, half, *refs):
    src, (packs, wy, wr, yb, top, bottom) = refs[:count], refs[count:]

    def put(k, v):
        yb[k] = v
        top[k] = v[:RIM]
        bottom[k] = v[BX - RIM :]

    y_filter(wy, wr, planes_of(*src, half=half), packs, put)


def x_first_kernel(count, half, *refs):
    src, (above, below, lx, xa, packs) = refs[:count], refs[count:]
    x_filter(lx, planes_of(*src, half=half), above, below, storer(xa))
    col_rims(planes_of(xa), packs)


def y_first(src, half, cols, wy, wr, **more):
    return call(functools.partial(y_first_kernel, len(src), half), [HALF, *ROWS],
                *src, cols, wy, wr, **more)


def x_first(src, half, rows, lx, **more):
    return call(functools.partial(x_first_kernel, len(src), half), [HALF, *COLS],
                *src, *rows, lx, **more)


def ratio_core(load, kf, kb, obs, out, sends):
    for t in range(BX // 16):
        cut = [slice(16 * t, 16 * t + 8), slice(16 * t + 8, 16 * t + 16)]
        blurred = z_filter(kf, jnp.concatenate([load(c) for c in cut], axis=1))
        seen = jnp.concatenate([obs[:, c, :].reshape(256, BY) for c in cut], axis=1)
        back = z_filter(kb, seen / blurred)
        for i, c in enumerate(cut):
            out[:, c, :] = back[:, i * BY : (i + 1) * BY].reshape(Z, 8, BY)
    x = lax.axis_index("view") // 2
    for j, send in zip(partners(), sends):
        send[:512] = out[pl.ds(8 * (x ^ j), 8)].reshape(512, BY)


def second_y_kernel(xa, packs, wy, wr, out):
    y_filter(wy, wr, planes_of(xa), packs, storer(out))


def ratio_start_kernel(ga, yb, above, below, lx, kf, kb, obs, note, s0, s1, s3, s2, out, gb):
    x_filter(lx, planes_of(yb), above, below, storer(gb))

    def load(c):
        return jnp.concatenate([ga[:, c, :], gb[:, c, :]], axis=0).reshape(256, BY)

    ratio_core(load, kf, kb, obs, out, (s0, s1, s3, s2))
    for send in (s1, s3, s2):
        send[512:] = note[...]


def ratio_kernel(g1, g3, g2, g0, kf, kb, obs, s0, s1, s3, s2, tmp, out):
    x = lax.axis_index("view") // 2
    for j, got in zip(partners(), (g0, g1, g3, g2)):
        tmp[pl.ds(8 * (x ^ j), 8)] = got[...].reshape(8, BX, BY)
    ratio_core(lambda c: tmp[:, c, :].reshape(256, BY), kf, kb, obs, out, (s0, s1, s3, s2))


SHARD, NOTED = sds(512, BY), sds(520, BY)
EDGE = sds(8, RIM, BY)
PACK = sds(4, BY, BY)
WHOLE = pltpu.VMEM((Z, BX, BY), F32)


def shard_cols_kernel(own, above, below, out):
    planes = [jnp.concatenate([above[k], own[k * BX : (k + 1) * BX], below[k]], axis=0)
              for k in range(8)]
    col_rims(planes, out)


def spread_kernel(picks, own, above, below, packs, *refs):
    count = len(picks)
    mats, outs, mid = refs[: 3 * count], refs[3 * count : -1], refs[-1]
    tiles = [jnp.concatenate([above[k], own[k * BX : (k + 1) * BX], below[k]], axis=0)
             for k in range(8)]
    tiles += [packs[k] for k in range(4)]
    for g in range(6):
        hi, lo = split(jnp.concatenate(tiles[2 * g : 2 * g + 2], axis=1))
        both = jnp.concatenate([hi, lo], axis=0)
        for n in range(count):
            o = dot(mats[3 * n][picks[n]], both)
            o = o[:BX] + o[BX:]
            mid[n, 2 * g] = o[:, :BY]
            mid[n, 2 * g + 1] = o[:, BY:]
    for n in range(count):
        out = outs[n]

        def put(k, v, out=out):
            out[k * BX : (k + 1) * BX] = v

        y_filter(mats[3 * n + 1].at[picks[n]], mats[3 * n + 2].at[picks[n]],
                 [mid[n, k] for k in range(8)], [mid[n, 8 + k] for k in range(4)], put)


def spread(picks, new, got, packs, mats, **more):
    return call(functools.partial(spread_kernel, picks), [SHARD] * len(picks),
                new, *got, packs, *mats, **more,
                scratch=[pltpu.VMEM((len(picks), 12, BX, BY), F32)])


def collect_columns(r, w, rims, put):
    for g in range(2):
        planes = [r[(4 * g + q) * BX : (4 * g + q + 1) * BX] for q in range(4)]
        hi, lo = split(jnp.concatenate(planes, axis=0))
        o = dot_turned(hi, w[:, :BY]) + dot_turned(hi, w[:, BY:]) + dot_turned(lo, w[:, :BY])
        for q in range(4):
            put(4 * g + q, o[q * BX : (q + 1) * BX])
        pairs = [jnp.concatenate(planes[2 * i : 2 * i + 2], axis=1) for i in range(2)]
        hi, lo = split(jnp.concatenate(pairs, axis=0))
        e = dot_turned(hi, rims[0]) + dot_turned(hi, rims[1]) + dot_turned(lo, rims[0])
        for i in range(2):
            put(8 + 2 * g + i, e[i * BX : (i + 1) * BX])


def collect_first_kernel(r0, r1, r3, wy, wr, mid):
    for j, r in enumerate((r0, r1, r3)):
        def put(k, v, j=j):
            mid[k, j * BX : (j + 1) * BX] = v

        collect_columns(r, wy.at[j], wr.at[j], put)


def collect_kernel(part, r2, wy, wr, lt, main, packs, late):
    def put_late(k, v):
        late[k] = v

    collect_columns(r2, wy.at[0], wr.at[0], put_late)
    for g in range(6):
        both = [jnp.concatenate([part[k], late[k]], axis=0) for k in (2 * g, 2 * g + 1)]
        hi, lo = split(jnp.concatenate(both, axis=1))
        o = dot(lt[0], hi) + dot(lt[0], lo) + dot(lt[1], hi)
        for i in range(2):
            k = 2 * g + i
            v = o[:, i * BY : (i + 1) * BY]
            if k < 8:
                main[k] = v
            else:
                packs[k - 8] = v


def add_cols_kernel(main, packs, own, up, down):
    near = lanes((BY, BY)) < BY // 2
    for k in range(8):
        pack = packs[k // 2]
        side = pltpu.roll(pack, BY // 2, 1) if k % 2 else pack
        v = main[k] + jnp.where(near, side, 0.0)
        up[k] = v[:RIM]
        own[k * BX : (k + 1) * BX] = v[RIM : RIM + BX]
        down[k] = v[RIM + BX :]


def add_rows_kernel(own, above, below, *refs):
    out, notes = refs[-1], refs[:-1]
    for k in range(8):
        r = k * BX
        out[r : r + RIM] = own[r : r + RIM] + above[k]
        out[r + RIM : r + BX] = own[r + RIM : r + BX] + below[k]
    for j, note in enumerate(notes):
        out[512 + 8 * j : 520 + 8 * j] = note[...] if j == 0 else note[512:]


def touch_kernel(out):
    out[...] = jnp.zeros_like(out)


def update_kernel(first, *refs):
    if first:
        f, mine, other, out, weight, top, bottom, turned = refs
    else:
        f, mine, other, weight, out = refs
    x = lax.axis_index("view") // 2
    if first:
        every = jnp.concatenate(
            [mine[512:], other[512:], jnp.zeros((64, 128), F32)], axis=0)
        turned[...] = jnp.transpose(every)
        outer = []
        for v in range(8):
            outer.append(turned[:BX, 8 * v + 4 : 8 * v + 5] * every[8 * v + 5 : 8 * v + 6])
        late = x >= 2
        for k in range(8):
            z_row = turned[pl.ds(pl.multiple_of(64 * (x % 2) + 8 * k, 8), 1), :]
            total = None
            for v in range(8):
                c = 8 * v + 6
                term = jnp.where(late, z_row[:, c + 1 : c + 2], z_row[:, c : c + 1]) * outer[v]
                total = term if total is None else total + term
            weight[k * BX : (k + 1) * BX] = total
        old = f[pl.ds(8 * x, 8)].reshape(512, BY)
    else:
        old = f[...]
    new = old * (mine[:512] + other[:512]) / weight[...]
    out[...] = new
    if first:
        for k in range(8):
            top[k] = new[k * BX : k * BX + RIM]
            bottom[k] = new[(k + 1) * BX - RIM : (k + 1) * BX]


def gather_kernel(own, one, three, two, f):
    x = lax.axis_index("view") // 2
    for j, ref in zip(partners(), (own, one, three, two)):
        f[pl.ds(8 * (x ^ j), 8)] = ref[...].reshape(8, BX, BY)


def cols_kernel(offs, obs, packs, out, top, bottom):
    shift = offs[0, 1] + RIM
    outside = lanes((BX, BY)) + shift >= BY
    for k in range(Z):
        own = pltpu.roll(obs[k], BY - shift, 1)
        side = pltpu.roll(packs[k // 2], lax.rem(2 * BY - shift - BY // 2 * (k % 2), BY), 1)
        v = jnp.where(outside, side, own)
        out[k] = v
        top[k] = v[:SHIFT]
        bottom[k] = v[BX - SHIFT :]


def rows_kernel(offs, obs, above, below, out):
    ox = offs[0, 0]
    total = BX + 2 * SHIFT
    amount = lax.rem(2 * total - SHIFT - ox, total)
    for k in range(Z):
        wide = jnp.concatenate([above[k], obs[k], below[k]], axis=0)
        out[k] = pltpu.roll(wide, amount, 0)[:BX]


def along_rows(x, by):
    return lax.ppermute(x, "blk", [(i, (i + 4 * by) % 32) for i in range(32)])


def along_cols(x, by):
    return lax.ppermute(x, "blk", [(i, i // 4 * 4 + (i + by) % 4) for i in range(32)])


def view_swap(x, mask):
    return lax.ppermute(x, "view", [(i, i ^ mask) for i in range(8)])


def send_rows(top, bottom):
    return along_rows(bottom, 1), along_rows(top, -1)


def trade(own, one, three, two):
    def swap(x, even, odd):
        pairs = [(v * 32 + b, (v ^ (2 * (odd if b % 2 else even))) * 32 + b)
                 for v in range(8) for b in range(32)]
        return lax.ppermute(x, ("view", "blk"), pairs)

    return own, swap(one, 1, 3), swap(three, 3, 1), swap(two, 2, 2)


def local(estimate, observed, kernels, offsets):
    f = estimate[0]
    seen = observed[0, 0]
    packs = call(functools.partial(col_rims_kernel, 1), COLS, f)
    cols_b = along_cols(packs, -1)
    edges = call(functools.partial(row_rims_kernel, 0), ROWS, f, before=(packs,))
    rows_a = send_rows(*edges)
    lxf, wyf, wrf, kzf, kzb, note = own_matrices(offsets, kernels, before=edges[:1])
    obs_packs = call(obs_cols_kernel, [sds(Z // 2, BX, BY)], seen, before=edges[:1])
    obs_cols = along_cols(obs_packs, -1)
    obs, top, bottom = call(
        cols_kernel, [sds(Z, BX, BY), sds(Z, SHIFT, BY), sds(Z, SHIFT, BY)],
        offsets, seen, obs_cols, smem=(0,))
    above, below = send_rows(top, bottom)
    xa, packs = x_first((f,), 0, rows_a, lxf, before=(obs,))
    cols_a = along_cols(packs, -1)
    yb, *rims = y_first((f,), 1, cols_b, wyf, wrf, before=(xa,))
    rows_b = send_rows(*rims)
    obs = call(rows_kernel, [sds(Z, BX, BY)], offsets, obs, above, below, smem=(0,),
               before=(yb,))
    ga = call(second_y_kernel, [HALF], xa, cols_a, wyf, wrf, before=(obs,))
    parts = call(ratio_start_kernel, [SHARD] + [NOTED] * 3, ga, yb, *rows_b, lxf, kzf, kzb,
                 obs, note, scratch=[WHOLE, pltpu.VMEM((HALF_Z, BX, BY), F32)])
    for step in range(ITERS):
        first = step == 0
        if not first:
            got = send_rows(top, bottom)
            packs = along_cols(call(shard_cols_kernel, [PACK], new, *got), -1)
            one, three = spread((1, 2), new, got, packs, [*near[:3], *near[:3]])
            two, own = spread((0, 0), new, got, packs, [*far[:3], *near[:3]], after=(one,))
            own, one, three, two = trade(own, one, three, two)
            mark = call(touch_kernel, [sds(8, BY)], before=(one, three))
            parts = call(ratio_kernel, [SHARD] * 4, one, three, two, own, kzf, kzb, obs,
                         before=(mark,), scratch=[WHOLE, WHOLE])
        own, one, three, two = trade(*parts)
        if first:
            near = call(near_matrices_kernel, many(3), note, one, three, scratch=TAP_SCRATCH)
            notes = (note, one, three, two)
        part = call(collect_first_kernel, [sds(12, 192, BY)], own, one, three, *near[1:3])
        if first:
            far = call(far_matrices_kernel, many(1), two, near[3], before=(part,),
                       scratch=TAP_SCRATCH)
        main, packs = call(collect_kernel, [sds(8, BY, BY), PACK], part, two, *far[1:],
                           scratch=[pltpu.VMEM((12, BX, BY), F32)])
        own, up, down = call(add_cols_kernel, [sds(512, BY), EDGE, EDGE],
                             main, along_cols(packs, 1))
        extra = notes if first else ()
        mine = call(add_rows_kernel, [sds(512 + 8 * len(extra), BY)],
                    own, *send_rows(up, down), *extra)
        other = view_swap(mine, 1)
        if first:
            new, weight, top, bottom = call(
                functools.partial(update_kernel, True),
                [sds(512, BY), sds(512, BY), EDGE, EDGE],
                f, mine, other, scratch=[pltpu.VMEM((128, 128), F32)])
        else:
            new = call(functools.partial(update_kernel, False), [sds(512, BY)],
                       new, mine, other, weight)
    return call(gather_kernel, [sds(Z, BX, BY)], *trade(new, new, new, new))[None]


def solution(mesh):
    in_specs = (
        P("blk", None, None, None),
        P("view", "blk", None, None, None),
        P("view", None, None),
        P("view", None),
    )
    out_specs = P("blk", None, None, None)
    return jax.shard_map(local, mesh=mesh, in_specs=in_specs, out_specs=out_specs, check_vma=False)
```

```python
import functools
import jax
import jax.numpy as jnp
from jax import lax
from jax.experimental import pallas as pl
from jax.experimental.pallas import tpu as pltpu
from jax.sharding import PartitionSpec as P

TAPS = 63
ITERS = 2
Z, BX, BY = 32, 64, 128
HALF_Z = Z // 2
RIM = 32
SHIFT = 16
GRID = 512
F32, BF16 = jnp.float32, jnp.bfloat16
PROF = 8


def split(x):
    hi = x.astype(BF16)
    return hi, (x - hi.astype(F32)).astype(BF16)


def dot(a, b):
    return jnp.dot(a, b, preferred_element_type=F32)


def wrap_of(pos):
    return jnp.where(pos >= GRID, 1, 0) - jnp.where(pos < 0, 1, 0)


def sds(*shape, dtype=F32):
    return jax.ShapeDtypeStruct(shape, dtype)


def call(body, out_shape, *args, smem=(), before=(), after=(), scratch=(), flops=1_000_000):
    specs = [
        pl.BlockSpec(memory_space=pltpu.SMEM if i in smem else pltpu.VMEM)
        for i in range(len(args))
    ]
    count, lead, tail = len(args), len(before), len(after)

    def inner(*refs):
        body(*refs[lead : lead + count], *refs[lead + count + tail :])

    loose = pl.BlockSpec(memory_space=pl.ANY)
    specs = [loose] * lead + specs + [loose] * tail
    size = sum(v.size * v.dtype.itemsize for v in (*args, *out_shape))
    outs = pl.pallas_call(
        inner,
        out_shape=out_shape,
        in_specs=specs,
        out_specs=[pl.BlockSpec(memory_space=pltpu.VMEM) for _ in out_shape],
        scratch_shapes=list(scratch),
        compiler_params=pltpu.CompilerParams(vmem_limit_bytes=40 * 1024 * 1024),
        cost_estimate=pl.CostEstimate(flops=flops, bytes_accessed=size, transcendentals=0),
    )(*before, *args, *after)
    return outs if len(outs) > 1 else outs[0]


def even_column():
    return lax.axis_index("blk") % 2 == 0


def partners():
    core = lax.axis_index("blk") % 2
    return 0, 1 + 2 * core, 3 - 2 * core, 2


def lanes(shape):
    return lax.broadcasted_iota(jnp.int32, shape, len(shape) - 1)


def rows_of(shape):
    return lax.broadcasted_iota(jnp.int32, shape, len(shape) - 2)


def tap_rows(taps, full, rows, depth=True):
    full[...] = jnp.zeros_like(full)
    full[:3, :TAPS] = taps
    x = full[...]
    hi, lo = split(x)
    mid, low = split(x - hi.astype(F32))
    parts = jnp.concatenate([hi, mid, low, jnp.zeros_like(hi)], axis=0)

    def moved(step, flip, width):
        j = lax.broadcasted_iota(jnp.int32, (BY, width), 0)
        target = (TAPS - 1 - j if flip else j) * step
        hot = jnp.where((lanes((BY, width)) == target) & (j < TAPS), 1.0, 0.0).astype(BF16)
        out = dot(parts, hot)
        return out[:8] + (out[8:16] + out[16:24])

    rows[...] = jnp.zeros_like(rows)
    flipped = moved(1, True, BY)
    rows[0:1, :BY] = x[0:1]
    rows[1:2, :BY] = flipped[0:1]
    rows[2:3, :BY] = x[1:2]
    rows[3:4, :BY] = flipped[1:2]
    if depth:
        rows[4:5, :512] = moved(8, False, 512)[2:3]
        rows[5:6, :512] = moved(8, True, 512)[2:3]


def block_start():
    block = lax.axis_index("blk")
    return (block // 4) * BX, (block % 4) * BY


def x_band(rows, row, s, ox, adjoint=False):
    base = jnp.broadcast_to(rows[row : row + 1, :BY], (BX, BY))
    band = pltpu.roll(base, 1, 1, stride=1, stride_axis=0)
    m = s + lanes((BX, BY)) - RIM
    i = s + ox + rows_of((BX, BY))
    keep = (wrap_of(m + ox) == 0) if adjoint else (wrap_of(i) == wrap_of(m))
    return jnp.where(keep, band, 0.0)


def x_band_turned(rows, row, s, ox):
    base = jnp.broadcast_to(rows[row : row + 1, :256], (BY, 256))
    band = pltpu.roll(base, 193, 1, stride=1, stride_axis=0)[:, :BY]
    m = s + rows_of((BY, BY)) - RIM
    i = s + ox + lanes((BY, BY))
    keep = (wrap_of(i) == wrap_of(m)) & (lanes((BY, BY)) < BX)
    return jnp.where(keep, band, 0.0)[:, :BX]


def y_toeplitz(rows, row):
    base = jnp.broadcast_to(rows[row : row + 1, :256], (BY + 2 * RIM, 256))
    return pltpu.roll(base, 193, 1, stride=1, stride_axis=0)[:, :BY]


def y_band(rows, row, cs, oy):
    band = y_toeplitz(rows, row)
    m = cs + rows_of(band.shape)
    j = cs + oy + RIM + lanes(band.shape)
    return jnp.where(wrap_of(j) == wrap_of(m), band, 0.0)


def y_profile(rows, row, cs, oy):
    band = y_toeplitz(rows, row)
    m = cs + rows_of(band.shape) - RIM
    return jnp.sum(jnp.where(wrap_of(m + oy) == 0, band, 0.0), axis=0, keepdims=True)


def z_band(rows, row, shift):
    amount = lax.rem(1024 - 248 - 8 * shift, 1024)
    moved = pltpu.roll(rows[...], amount, 1)[row : row + 1]
    base = jnp.broadcast_to(moved, (256, 1024))
    return pltpu.roll(base, 0, 1, stride=1, stride_axis=0)[:, :256]


def put_x(ref, band):
    hi, lo = split(band)
    top = jnp.concatenate([hi, hi], axis=1)
    bottom = jnp.concatenate([lo, jnp.zeros_like(lo)], axis=1)
    ref[...] = jnp.concatenate([top, bottom], axis=0)


def put_y(main, rims, band):
    hi, lo = split(band[:BY])
    main[...] = jnp.concatenate([hi, lo], axis=1)
    side = band[BY:]
    none = jnp.zeros_like(side)
    whole = jnp.concatenate([jnp.concatenate([side, none], axis=1),
                             jnp.concatenate([none, side], axis=1)], axis=0)
    rims[0], rims[1] = split(whole)


def own_kernel(offs, taps, lxf, wyf, wrf, kzf, kzb, note, full, rows):
    tap_rows(taps[0], full, rows)
    s, cs = block_start()
    ox, oy, oz = offs[0, 0], offs[0, 1], offs[0, 2]
    put_x(lxf, x_band(rows, 1, s, ox))
    put_y(wyf, wrf, y_band(rows, 2, cs, oy))
    front_z = z_band(rows, 5, oz)
    kzf[0], kzf[1] = split(front_z)
    kzb[0], kzb[1] = split(z_band(rows, 4, -oz))
    back_x = x_band(rows, 0, s, ox, True)
    turned = jnp.transpose(jnp.concatenate([back_x, jnp.zeros_like(back_x)], axis=0))
    prof_x = jnp.sum(turned, axis=0, keepdims=True)
    prof_y = y_profile(rows, 3, cs, oy)
    prof_z = jnp.sum(front_z, axis=0, keepdims=True)
    lane = lanes((1, BY))
    shifts = jnp.where(lane == 0, ox, jnp.where(lane == 1, oy, 0)).astype(F32)
    note[...] = jnp.concatenate(
        [full[:3], shifts, prof_x, prof_y, prof_z[:, :128], prof_z[:, 128:]], axis=0)


LX, WY = sds(128, 256, dtype=BF16), sds(128, 256, dtype=BF16)
WR, KZ = sds(2, 128, 256, dtype=BF16), sds(2, 256, 256, dtype=BF16)
LT = sds(2, 128, 256, dtype=BF16)
TAP_SCRATCH = [pltpu.VMEM((8, BY), F32), pltpu.VMEM((8, 1024), F32)]


def own_matrices(offs, taps, **more):
    return call(own_kernel, [LX, WY, WR, KZ, KZ, sds(PROF, 128)], offs, taps, smem=(0,),
                scratch=TAP_SCRATCH, **more)


def view_matrices(note, lx, wy, wr, lt, j, full, rows):
    s, cs = block_start()
    tap_rows(note[:3, :TAPS], full, rows, False)
    shifts = note[3:4]
    ox = shifts[:, 0:1].astype(jnp.int32)
    oy = shifts[:, 1:2].astype(jnp.int32)
    put_x(lx, x_band(rows, 1, s, ox))
    put_y(wy, wr, y_band(rows, 2, cs, oy))
    hi, lo = split(x_band_turned(rows, 0, s, ox))
    lt[0, :, j * BX : (j + 1) * BX] = hi
    lt[1, :, j * BX : (j + 1) * BX] = lo


def near_matrices_kernel(note, m1, m3, lx, wy, wr, lt, full, rows):
    lt[...] = jnp.zeros_like(lt)
    for j, ref in enumerate((note, m1, m3)):
        one = ref[...] if j == 0 else ref[512:]
        view_matrices(one, lx.at[j], wy.at[j], wr.at[j], lt, j, full, rows)


def far_matrices_kernel(m2, old, lx, wy, wr, lt, full, rows):
    lt[...] = old[...]
    view_matrices(m2[512:], lx.at[0], wy.at[0], wr.at[0], lt, 3, full, rows)


def many(count):
    return [sds(count, *v.shape, dtype=v.dtype) for v in (LX, WY, WR)] + [LT]


def row_rims(planes, top, bottom):
    for k, plane in enumerate(planes):
        top[k] = plane[:RIM]
        bottom[k] = plane[BX - RIM :]


def col_rims(planes, out):
    there = lanes(planes[0].shape) >= BY // 2
    for g in range(len(planes) // 2):
        out[g] = jnp.where(there, pltpu.roll(planes[2 * g + 1], BY // 2, 1), planes[2 * g])


ROWS = [sds(HALF_Z, RIM, BY), sds(HALF_Z, RIM, BY)]
COLS = [sds(HALF_Z // 2, BX, BY)]
HALF = sds(HALF_Z, BX, BY)


def planes_of(*refs, half=None):
    planes = []
    for ref in refs:
        if len(ref.shape) == 3:
            skip = 0 if half is None else half * HALF_Z
            stop = ref.shape[0] if half is None else skip + HALF_Z
            planes += [ref[k] for k in range(skip, stop)]
        else:
            planes += [ref[k * BX : (k + 1) * BX] for k in range(ref.shape[0] // BX)]
    return planes


def row_rims_kernel(half, *refs):
    row_rims(planes_of(*refs[:-2], half=half), *refs[-2:])


def col_rims_kernel(half, *refs):
    col_rims(planes_of(*refs[:-1], half=half), refs[-1])


def obs_cols_kernel(obs, out):
    col_rims(planes_of(obs), out)


def x_filter(mat, own, above, below, put):
    for g in range(HALF_Z // 2):
        both = []
        for k in (2 * g, 2 * g + 1):
            both.append(jnp.concatenate([above[k], own[k], below[k]], axis=0))
        o = x_pair(mat, jnp.concatenate(both, axis=1))
        put(2 * g, o[:, :BY])
        put(2 * g + 1, o[:, BY:])


def x_pair(mat, wide):
    hi, lo = split(wide)
    o = dot(mat[...], jnp.concatenate([hi, lo], axis=0))
    return o[:BX] + o[BX:]


def y_filter(main, rims, own, packs, put):
    for g in range(len(own) // 4):
        x = jnp.concatenate([own[4 * g + q] for q in range(4)], axis=0)
        hi, lo = split(x)
        o = dot(hi, main[...])
        o = o[:, :BY] + o[:, BY:] + dot(lo, main[:, :BY])
        hi, lo = split(jnp.concatenate([packs[2 * g], packs[2 * g + 1]], axis=0))
        r = dot(hi, rims[0]) + dot(hi, rims[1]) + dot(lo, rims[0])
        for q in range(4):
            i = q // 2 * BX
            j = q % 2 * BY
            put(4 * g + q, o[q * BX : (q + 1) * BX] + r[i : i + BX, j : j + BY])


def dot_turned(a, b):
    return lax.dot_general(a, b, (((1,), (1,)), ((), ())), preferred_element_type=F32)


def z_filter(mat, tiles):
    hi, lo = split(tiles)
    return dot(mat[0], hi) + dot(mat[0], lo) + dot(mat[1], hi)


def storer(ref, place=lambda k: k):
    def put(k, v):
        ref[place(k)] = v

    return put


def y_first_kernel(count, half, *refs):
    src, (packs, wy, wr, yb, top, bottom) = refs[:count], refs[count:]

    def put(k, v):
        yb[k] = v
        top[k] = v[:RIM]
        bottom[k] = v[BX - RIM :]

    y_filter(wy, wr, planes_of(*src, half=half), packs, put)


def x_first_kernel(count, half, *refs):
    src, (above, below, lx, xa, packs) = refs[:count], refs[count:]
    x_filter(lx, planes_of(*src, half=half), above, below, storer(xa))
    col_rims(planes_of(xa), packs)


def y_first(src, half, cols, wy, wr, **more):
    return call(functools.partial(y_first_kernel, len(src), half), [HALF, *ROWS],
                *src, cols, wy, wr, **more)


def x_first(src, half, rows, lx, **more):
    return call(functools.partial(x_first_kernel, len(src), half), [HALF, *COLS],
                *src, *rows, lx, **more)


def ratio_core(load, kf, kb, obs, out, sends):
    for t in range(BX // 16):
        cut = [slice(16 * t, 16 * t + 8), slice(16 * t + 8, 16 * t + 16)]
        blurred = z_filter(kf, jnp.concatenate([load(c) for c in cut], axis=1))
        seen = jnp.concatenate([obs[:, c, :].reshape(256, BY) for c in cut], axis=1)
        back = z_filter(kb, seen / blurred)
        for i, c in enumerate(cut):
            out[:, c, :] = back[:, i * BY : (i + 1) * BY].reshape(Z, 8, BY)
    x = lax.axis_index("view") // 2
    for j, send in zip(partners(), sends):
        send[:512] = out[pl.ds(8 * (x ^ j), 8)].reshape(512, BY)


def second_y_kernel(xa, packs, wy, wr, out):
    y_filter(wy, wr, planes_of(xa), packs, storer(out))


def ratio_start_kernel(ga, yb, above, below, lx, kf, kb, obs, note, s0, s1, s3, s2, out, gb):
    x_filter(lx, planes_of(yb), above, below, storer(gb))

    def load(c):
        return jnp.concatenate([ga[:, c, :], gb[:, c, :]], axis=0).reshape(256, BY)

    ratio_core(load, kf, kb, obs, out, (s0, s1, s3, s2))
    for send in (s1, s3, s2):
        send[512:] = note[...]


def ratio_kernel(g1, g3, g2, g0, kf, kb, obs, s0, s1, s3, s2, tmp, out):
    x = lax.axis_index("view") // 2
    for j, got in zip(partners(), (g0, g1, g3, g2)):
        tmp[pl.ds(8 * (x ^ j), 8)] = got[...].reshape(8, BX, BY)
    ratio_core(lambda c: tmp[:, c, :].reshape(256, BY), kf, kb, obs, out, (s0, s1, s3, s2))


SHARD, NOTED = sds(512, BY), sds(520, BY)
EDGE = sds(8, RIM, BY)
PACK = sds(4, BY, BY)
WHOLE = pltpu.VMEM((Z, BX, BY), F32)


def shard_cols_kernel(own, above, below, out):
    planes = [jnp.concatenate([above[k], own[k * BX : (k + 1) * BX], below[k]], axis=0)
              for k in range(8)]
    col_rims(planes, out)


def spread_kernel(picks, own, above, below, packs, *refs):
    count = len(picks)
    mats, outs, mid = refs[: 3 * count], refs[3 * count : -1], refs[-1]
    tiles = [jnp.concatenate([above[k], own[k * BX : (k + 1) * BX], below[k]], axis=0)
             for k in range(8)]
    tiles += [packs[k] for k in range(4)]
    for g in range(6):
        hi, lo = split(jnp.concatenate(tiles[2 * g : 2 * g + 2], axis=1))
        both = jnp.concatenate([hi, lo], axis=0)
        for n in range(count):
            o = dot(mats[3 * n][picks[n]], both)
            o = o[:BX] + o[BX:]
            mid[n, 2 * g] = o[:, :BY]
            mid[n, 2 * g + 1] = o[:, BY:]
    for n in range(count):
        out = outs[n]

        def put(k, v, out=out):
            out[k * BX : (k + 1) * BX] = v

        y_filter(mats[3 * n + 1].at[picks[n]], mats[3 * n + 2].at[picks[n]],
                 [mid[n, k] for k in range(8)], [mid[n, 8 + k] for k in range(4)], put)


def spread(picks, new, got, packs, mats, **more):
    return call(functools.partial(spread_kernel, picks), [SHARD] * len(picks),
                new, *got, packs, *mats, **more,
                scratch=[pltpu.VMEM((len(picks), 12, BX, BY), F32)])


def collect_columns(r, w, rims, put):
    for g in range(2):
        planes = [r[(4 * g + q) * BX : (4 * g + q + 1) * BX] for q in range(4)]
        hi, lo = split(jnp.concatenate(planes, axis=0))
        o = dot_turned(hi, w[:, :BY]) + dot_turned(hi, w[:, BY:]) + dot_turned(lo, w[:, :BY])
        for q in range(4):
            put(4 * g + q, o[q * BX : (q + 1) * BX])
        pairs = [jnp.concatenate(planes[2 * i : 2 * i + 2], axis=1) for i in range(2)]
        hi, lo = split(jnp.concatenate(pairs, axis=0))
        e = dot_turned(hi, rims[0]) + dot_turned(hi, rims[1]) + dot_turned(lo, rims[0])
        for i in range(2):
            put(8 + 2 * g + i, e[i * BX : (i + 1) * BX])


def collect_first_kernel(r0, r1, r3, wy, wr, mid):
    for j, r in enumerate((r0, r1, r3)):
        def put(k, v, j=j):
            mid[k, j * BX : (j + 1) * BX] = v

        collect_columns(r, wy.at[j], wr.at[j], put)


def collect_kernel(part, r2, wy, wr, lt, main, packs, late):
    def put_late(k, v):
        late[k] = v

    collect_columns(r2, wy.at[0], wr.at[0], put_late)
    for g in range(6):
        both = [jnp.concatenate([part[k], late[k]], axis=0) for k in (2 * g, 2 * g + 1)]
        hi, lo = split(jnp.concatenate(both, axis=1))
        o = dot(lt[0], hi) + dot(lt[0], lo) + dot(lt[1], hi)
        for i in range(2):
            k = 2 * g + i
            v = o[:, i * BY : (i + 1) * BY]
            if k < 8:
                main[k] = v
            else:
                packs[k - 8] = v


def add_cols_kernel(main, packs, own, up, down):
    near = lanes((BY, BY)) < BY // 2
    for k in range(8):
        pack = packs[k // 2]
        side = pltpu.roll(pack, BY // 2, 1) if k % 2 else pack
        v = main[k] + jnp.where(near, side, 0.0)
        up[k] = v[:RIM]
        own[k * BX : (k + 1) * BX] = v[RIM : RIM + BX]
        down[k] = v[RIM + BX :]


def add_rows_kernel(own, above, below, *refs):
    out, notes = refs[-1], refs[:-1]
    for k in range(8):
        r = k * BX
        out[r : r + RIM] = own[r : r + RIM] + above[k]
        out[r + RIM : r + BX] = own[r + RIM : r + BX] + below[k]
    for j, note in enumerate(notes):
        out[512 + 8 * j : 520 + 8 * j] = note[...] if j == 0 else note[512:]


def touch_kernel(out):
    out[...] = jnp.zeros_like(out)


def update_kernel(first, *refs):
    if first:
        f, mine, other, out, weight, top, bottom, turned = refs
    else:
        f, mine, other, weight, out = refs
    x = lax.axis_index("view") // 2
    if first:
        every = jnp.concatenate(
            [mine[512:], other[512:], jnp.zeros((64, 128), F32)], axis=0)
        turned[...] = jnp.transpose(every)
        outer = []
        for v in range(8):
            outer.append(turned[:BX, 8 * v + 4 : 8 * v + 5] * every[8 * v + 5 : 8 * v + 6])
        late = x >= 2
        for k in range(8):
            z_row = turned[pl.ds(pl.multiple_of(64 * (x % 2) + 8 * k, 8), 1), :]
            total = None
            for v in range(8):
                c = 8 * v + 6
                term = jnp.where(late, z_row[:, c + 1 : c + 2], z_row[:, c : c + 1]) * outer[v]
                total = term if total is None else total + term
            weight[k * BX : (k + 1) * BX] = total
        old = f[pl.ds(8 * x, 8)].reshape(512, BY)
    else:
        old = f[...]
    new = old * (mine[:512] + other[:512]) / weight[...]
    out[...] = new
    if first:
        for k in range(8):
            top[k] = new[k * BX : k * BX + RIM]
            bottom[k] = new[(k + 1) * BX - RIM : (k + 1) * BX]


def gather_kernel(own, one, three, two, f):
    x = lax.axis_index("view") // 2
    for j, ref in zip(partners(), (own, one, three, two)):
        f[pl.ds(8 * (x ^ j), 8)] = ref[...].reshape(8, BX, BY)


def cols_kernel(offs, obs, packs, out, top, bottom):
    shift = offs[0, 1] + RIM
    outside = lanes((BX, BY)) + shift >= BY
    for k in range(Z):
        own = pltpu.roll(obs[k], BY - shift, 1)
        side = pltpu.roll(packs[k // 2], lax.rem(2 * BY - shift - BY // 2 * (k % 2), BY), 1)
        v = jnp.where(outside, side, own)
        out[k] = v
        top[k] = v[:SHIFT]
        bottom[k] = v[BX - SHIFT :]


def rows_kernel(offs, obs, above, below, out):
    ox = offs[0, 0]
    total = BX + 2 * SHIFT
    amount = lax.rem(2 * total - SHIFT - ox, total)
    for k in range(Z):
        wide = jnp.concatenate([above[k], obs[k], below[k]], axis=0)
        out[k] = pltpu.roll(wide, amount, 0)[:BX]


def along_rows(x, by):
    return lax.ppermute(x, "blk", [(i, (i + 4 * by) % 32) for i in range(32)])


def along_cols(x, by):
    return lax.ppermute(x, "blk", [(i, i // 4 * 4 + (i + by) % 4) for i in range(32)])


def view_swap(x, mask):
    return lax.ppermute(x, "view", [(i, i ^ mask) for i in range(8)])


def send_rows(top, bottom):
    return along_rows(bottom, 1), along_rows(top, -1)


def trade(own, one, three, two):
    def swap(x, even, odd):
        pairs = [(v * 32 + b, (v ^ (2 * (odd if b % 2 else even))) * 32 + b)
                 for v in range(8) for b in range(32)]
        return lax.ppermute(x, ("view", "blk"), pairs)

    return own, swap(one, 1, 3), swap(three, 3, 1), swap(two, 2, 2)


def local(estimate, observed, kernels, offsets):
    f = estimate[0]
    seen = observed[0, 0]
    packs = call(functools.partial(col_rims_kernel, 1), COLS, f)
    cols_b = along_cols(packs, -1)
    edges = call(functools.partial(row_rims_kernel, 0), ROWS, f, before=(packs,))
    rows_a = send_rows(*edges)
    lxf, wyf, wrf, kzf, kzb, note = own_matrices(offsets, kernels, before=edges[:1])
    obs_packs = call(obs_cols_kernel, [sds(Z // 2, BX, BY)], seen, before=edges[:1])
    obs_cols = along_cols(obs_packs, -1)
    obs, top, bottom = call(
        cols_kernel, [sds(Z, BX, BY), sds(Z, SHIFT, BY), sds(Z, SHIFT, BY)],
        offsets, seen, obs_cols, smem=(0,))
    above, below = send_rows(top, bottom)
    xa, packs = x_first((f,), 0, rows_a, lxf, before=(obs,))
    cols_a = along_cols(packs, -1)
    yb, *rims = y_first((f,), 1, cols_b, wyf, wrf, before=(xa,))
    rows_b = send_rows(*rims)
    obs = call(rows_kernel, [sds(Z, BX, BY)], offsets, obs, above, below, smem=(0,),
               before=(yb,))
    ga = call(second_y_kernel, [HALF], xa, cols_a, wyf, wrf, before=(obs,))
    parts = call(ratio_start_kernel, [SHARD] + [NOTED] * 3, ga, yb, *rows_b, lxf, kzf, kzb,
                 obs, note, scratch=[WHOLE, pltpu.VMEM((HALF_Z, BX, BY), F32)])
    for step in range(ITERS):
        first = step == 0
        if not first:
            got = send_rows(top, bottom)
            packs = along_cols(call(shard_cols_kernel, [PACK], new, *got), -1)
            one, three = spread((1, 2), new, got, packs, [*near[:3], *near[:3]])
            two = spread((0,), new, got, packs, far[:3], after=(one,))
            own = spread((0,), new, got, packs, near[:3], after=(two,))
            own, one, three, two = trade(own, one, three, two)
            mark = call(touch_kernel, [sds(8, BY)], before=(one, three))
            parts = call(ratio_kernel, [SHARD] * 4, one, three, two, own, kzf, kzb, obs,
                         before=(mark,), scratch=[WHOLE, WHOLE])
        own, one, three, two = trade(*parts)
        if first:
            near = call(near_matrices_kernel, many(3), note, one, three, scratch=TAP_SCRATCH)
            notes = (note, one, three, two)
        part = call(collect_first_kernel, [sds(12, 192, BY)], own, one, three, *near[1:3])
        if first:
            far = call(far_matrices_kernel, many(1), two, near[3], before=(part,),
                       scratch=TAP_SCRATCH)
        main, packs = call(collect_kernel, [sds(8, BY, BY), PACK], part, two, *far[1:],
                           scratch=[pltpu.VMEM((12, BX, BY), F32)])
        own, up, down = call(add_cols_kernel, [sds(512, BY), EDGE, EDGE],
                             main, along_cols(packs, 1))
        extra = notes if first else ()
        mine = call(add_rows_kernel, [sds(512 + 8 * len(extra), BY)],
                    own, *send_rows(up, down), *extra)
        other = view_swap(mine, 1)
        if first:
            new, weight, top, bottom = call(
                functools.partial(update_kernel, True),
                [sds(512, BY), sds(512, BY), EDGE, EDGE],
                f, mine, other, scratch=[pltpu.VMEM((128, 128), F32)])
        else:
            new = call(functools.partial(update_kernel, False), [sds(512, BY)],
                       new, mine, other, weight)
    return call(gather_kernel, [sds(Z, BX, BY)], *trade(new, new, new, new))[None]


def solution(mesh):
    in_specs = (
        P("blk", None, None, None),
        P("view", "blk", None, None, None),
        P("view", None, None),
        P("view", None),
    )
    out_specs = P("blk", None, None, None)
    return jax.shard_map(local, mesh=mesh, in_specs=in_specs, out_specs=out_specs, check_vma=False)
```
